256 devices in a mesh: section: 4 (over y), expert: 64 (over z, x, core).
Axes of the slice: x: 4, y: 4, z: 8, core: 2. Of those that a mesh axis runs over, the one named last changes fastest.
Arguments:
- inputs: bfloat16 [1, 2048, 2048], P(None, 'expert'), may hold values from -6 to 6
- norm_gain: float32 [4, 2048], P('section'), may hold values from 0.25 to 1.75
- expert_ids: int32 [4, 1, 2048, 2], P('section', None, 'expert'), may hold values from 0 to 63, all different within a row; in each aligned block of 32 rows (0 to 31, 32 to 63, ..., all dimensions but the last counted through in order) at most 2 rows name the same one
- route_weights: float32 [4, 1, 2048, 2], P('section', None, 'expert'), may hold values from 0.3 to 1
- gate_codes: bfloat16 [4, 64, 2048, 768], P('section', 'expert'), may hold values from 0 to 3, as said below
- up_codes: bfloat16 [4, 64, 2048, 768], P('section', 'expert'), may hold values from 0 to 3, as said below
- down_codes: bfloat16 [4, 64, 768, 2048], P('section', 'expert'), may hold values from 0 to 3, as said below
- gate_steps: float32 [4, 64, 32, 768], P('section', 'expert'), may hold values from 0.5 to 2
- up_steps: float32 [4, 64, 32, 768], P('section', 'expert'), may hold values from 0.5 to 2
- down_steps: float32 [4, 64, 12, 2048], P('section', 'expert'), may hold values from 0.5 to 2
- out_grad: bfloat16 [1, 2048, 2048], P(None, 'expert'), may hold values from -6 to 6
Outputs:
- layer_outputs: bfloat16 [4, 1, 2048, 2048], P('section', None, 'expert')
- input_grads: bfloat16 [4, 1, 2048, 2048], P('section', None, 'expert')
- gate_step_grads: float32 [4, 64, 32, 768], P('section', 'expert')
- up_step_grads: float32 [4, 64, 32, 768], P('section', 'expert')
- down_step_grads: float32 [4, 64, 12, 2048], P('section', 'expert')
The draws below stay inside these ranges and needn't reach their ends.
Inputs may be any that keep to these rules, and one draw needn't show every extreme that they name: `expert_ids`: each token names 2 different experts. Within one layer and one micro-batch, at most 2 of the 32 tokens of one device (aligned blocks of 32 tokens) name any one expert; the bound is reached in some of these blocks. `gate_codes`: integer codes. `up_codes`: integer codes. `down_codes`: integer codes.
All inputs are finite; a program needn't handle non-finite values.
Results may differ from the reference program's by a relative error of at most 0.028.
Values may be sent and summed in bfloat16 or wider, within the bound.
A program may use at most 128 MiB of HBM per device.

```python
import math
import jax
import jax.numpy as jnp
import numpy as np
from jax import lax

D = 2048
FF = 768
GROUP = 64
TOP = 2
MICRO = 1
TOK_DEV = 32
EXPERTS = 64
LAYERS = 4
TOKENS = 2048
MOST = 2
RECV = 128
N_EXPERT = 64


def draw_gate_codes(key, part):
    key = jax.random.fold_in(key, 11)
    values = jnp.floor(jax.random.uniform(key, (LAYERS, EXPERTS, D, FF), jnp.float32) * 4.0)
    return jnp.clip(values, 0.0, 3.0).astype(jnp.bfloat16)


def draw_up_codes(key, part):
    key = jax.random.fold_in(key, 12)
    values = jnp.floor(jax.random.uniform(key, (LAYERS, EXPERTS, D, FF), jnp.float32) * 4.0)
    return jnp.clip(values, 0.0, 3.0).astype(jnp.bfloat16)


def draw_down_codes(key, part):
    key = jax.random.fold_in(key, 13)
    values = jnp.floor(jax.random.uniform(key, (LAYERS, EXPERTS, FF, D), jnp.float32) * 4.0)
    return jnp.clip(values, 0.0, 3.0).astype(jnp.bfloat16)


def level_of(own_key, dims, cuts, low, top_value):
    factor_of, own = 1.0, jax.random.fold_in(own_key, 6)
    for dim, shards_of in cuts:
        draws = jnp.exp(jax.random.uniform(jax.random.fold_in(own, dim), (shards_of,), jnp.float32, low / len(cuts), top_value / len(cuts)))
        factor_of = factor_of * jnp.repeat(draws, dims[dim] // shards_of).reshape([-1 if axis == dim else 1 for axis in range(len(dims))])
    return factor_of


def routed_block(own_key, own, number, rows, number_of, top, limit, skew):
    ranking = jax.random.permutation(own_key, number_of)
    heavy_load, usual = shares(number_of, rows * top, limit, skew, True), shares(number_of, rows * top, limit, skew, False)
    places = jnp.arange(number_of)

    def named(tallies, turn):
        used = int((tallies > 0).sum())
        fixed = max(1, used // 4)
        shifted = fixed + (places - fixed + turn * (used - fixed)) % max(1, number_of - fixed)
        return jnp.zeros((number_of,), jnp.int32).at[ranking[jnp.where(places < fixed, places, shifted)]].set(jnp.asarray(tallies, jnp.int32))

    tallies = jnp.where(number % 4 == 0, named(heavy_load, number // 4), named(usual, number - number // 4 - 1))
    mixed = jax.random.permutation(jax.random.fold_in(own, 3), number_of)
    source_of, receiver = mixed[0:number_of // 2 * 2:2], mixed[1:number_of // 2 * 2:2]
    room = jnp.minimum(tallies[source_of] - 1, limit - tallies[receiver]) // 2
    room = jnp.where((source_of == ranking[0]) | (receiver == ranking[0]) | (tallies[receiver] == 0), 0, jnp.maximum(room, 0))
    shifted = jax.random.randint(jax.random.fold_in(own, 4), (number_of // 2,), 0, 1 << 20) % (room + 1)
    tallies = tallies.at[source_of].add(-shifted).at[receiver].add(shifted)
    labels = jnp.searchsorted(jnp.cumsum(tallies), jnp.arange(rows * top), side="right").astype(jnp.int32)
    grid = labels.reshape(top, rows).T
    grid = grid[jax.random.permutation(jax.random.fold_in(own, 1), rows)]
    turn = jax.random.randint(jax.random.fold_in(own, 2), (rows, 1), 0, top)
    return jnp.take_along_axis(grid, (jnp.arange(top)[None, :] + turn) % top, axis=1)


def shares(number_of, total, bound, skew, full):
    weights = [(1 << 20) // math.isqrt(rank ** skew) + 1 for rank in range(1, number_of + 1)]
    largest = bound if full else min(bound, max(-(-total // number_of), total * weights[0] // sum(weights)))
    least = 1 if total - largest >= number_of - 1 else 0
    counts, surplus = [largest] + [least] * (number_of - 1), total - largest - least * (number_of - 1)
    while surplus > 0:
        candidates = [i for i in range(1, number_of) if counts[i] < largest] or [i for i in range(1, number_of) if counts[i] < bound]
        mass, left = sum([weights[i] for i in candidates]), surplus
        for i in candidates:
            extra = min(bound - counts[i], max(1, left * weights[i] // mass), surplus)
            counts[i] = counts[i] + extra
            surplus = surplus - extra
    return np.array(counts)


def scatter_about(own_key, shape, width, bound, pieces=(), kind=jnp.bfloat16):
    entries = width * jax.random.normal(own_key, shape, jnp.float32)
    if pieces:
        entries = entries * level_of(own_key, shape, pieces, -0.22, 0.18)
    return jnp.clip(entries, -bound, bound).astype(kind)


def setup_inputs(seed: int = 0) -> dict:
    keys = jax.random.split(jax.random.key(seed), 12)
    inputs = scatter_about(keys[0], (MICRO, TOKENS, D), 1.0, 6.0, ((1, 64),))
    norm_gain = jnp.clip(1.0 + 0.15 * jax.random.normal(keys[1], (LAYERS, D), jnp.float32), 0.25, 1.75)
    expert_ids_keys = jax.random.split(jax.random.fold_in(keys[2], 1), LAYERS * MICRO * TOKENS // TOK_DEV)
    expert_ids_turns = jax.random.permutation(jax.random.fold_in(keys[2], 3), LAYERS * MICRO * TOKENS // TOK_DEV)
    expert_ids = jax.vmap(lambda own, number: routed_block(jax.random.fold_in(keys[2], 2), own, number, TOK_DEV, EXPERTS, TOP, MOST, 2))(expert_ids_keys, expert_ids_turns).reshape((LAYERS, MICRO, TOKENS, TOP))
    route_weights = jnp.clip(0.3 + 0.7 * jax.random.uniform(keys[3], (LAYERS, MICRO, TOKENS, TOP), jnp.float32) ** level_of(keys[3], (LAYERS, MICRO, TOKENS, TOP), ((0, 4), (2, 64)), -0.2, 0.2), 0.3, 1.0)
    gate_codes = draw_gate_codes(jax.random.fold_in(keys[11], 71), 0)
    up_codes = draw_up_codes(jax.random.fold_in(keys[11], 71), 0)
    down_codes = draw_down_codes(jax.random.fold_in(keys[11], 71), 0)
    gate_steps = jnp.clip(jnp.exp(math.log(2.0) - 1.3862944 * jax.random.uniform(keys[7], (LAYERS, EXPERTS, D // GROUP, FF), jnp.float32) ** level_of(keys[7], (LAYERS, EXPERTS, D // GROUP, FF), ((0, 4), (1, 64)), -0.2, 0.2)), 0.5, 2.0)
    up_steps = jnp.clip(jnp.exp(math.log(2.0) - 1.3862944 * jax.random.uniform(keys[8], (LAYERS, EXPERTS, D // GROUP, FF), jnp.float32) ** level_of(keys[8], (LAYERS, EXPERTS, D // GROUP, FF), ((0, 4), (1, 64)), -0.2, 0.2)), 0.5, 2.0)
    down_steps = jnp.clip(jnp.exp(math.log(2.0) - 1.3862944 * jax.random.uniform(keys[9], (LAYERS, EXPERTS, FF // GROUP, D), jnp.float32) ** level_of(keys[9], (LAYERS, EXPERTS, FF // GROUP, D), ((0, 4), (1, 64)), -0.2, 0.2)), 0.5, 2.0)
    out_grad = scatter_about(keys[10], (MICRO, TOKENS, D), 1.0, 6.0, ((1, 64),))
    return dict(inputs=inputs, norm_gain=norm_gain, expert_ids=expert_ids, route_weights=route_weights, gate_codes=gate_codes, up_codes=up_codes, down_codes=down_codes, gate_steps=gate_steps, up_steps=up_steps, down_steps=down_steps, out_grad=out_grad)


def dequant(codes, steps, fan_in):
    groups = steps.shape[0]
    shaped = codes.astype(jnp.float32).reshape(groups, -1, codes.shape[1]) - 1.5
    return (steps[:, None, :] * shaped * fan_in ** (-0.5)).reshape(codes.shape).astype(jnp.bfloat16)

def normalize(hidden, gain_row):
    hidden_f = hidden.astype(jnp.float32)
    inv_rms = lax.rsqrt(lax.optimization_barrier(jnp.mean(hidden_f * hidden_f, axis=-1, keepdims=True)) + 1e-06)
    return ((hidden_f * inv_rms * gain_row).astype(jnp.bfloat16), inv_rms)

def expert_gates(arrived, w_gate, w_up):
    gate_pre = jnp.dot(arrived, w_gate, preferred_element_type=jnp.float32)
    up_pre = jnp.dot(arrived, w_up, preferred_element_type=jnp.float32)
    return (gate_pre, up_pre)

def expert_forward(arrived, w_gate, w_up, w_down):
    gate_pre, up_pre = expert_gates(arrived, w_gate, w_up)
    silu_value = gate_pre * jax.nn.sigmoid(gate_pre)
    activated = (silu_value * up_pre).astype(jnp.bfloat16)
    result = jnp.dot(activated, w_down, preferred_element_type=jnp.float32).astype(jnp.bfloat16)
    return (result, gate_pre, up_pre)

def expert_backward(arrived_cot, gate_pre, up_pre, w_gate, w_up, w_down):
    contract = (((1,), (1,)), ((), ()))
    act_cot = lax.dot_general(arrived_cot, w_down, contract, preferred_element_type=jnp.float32)
    sigmoid_g = jax.nn.sigmoid(gate_pre)
    silu_value = gate_pre * sigmoid_g
    gate_cot = (act_cot * up_pre * sigmoid_g * (1.0 + gate_pre * (1.0 - sigmoid_g))).astype(jnp.bfloat16)
    up_cot = (act_cot * silu_value).astype(jnp.bfloat16)
    activated = (silu_value * up_pre).astype(jnp.bfloat16)
    row_grad = lax.dot_general(gate_cot, w_gate, contract, preferred_element_type=jnp.float32)
    row_grad = row_grad + lax.dot_general(up_cot, w_up, contract, preferred_element_type=jnp.float32)
    return (row_grad.astype(jnp.bfloat16), gate_cot, up_cot, activated)

def step_grad(weight_grad, codes, groups, fan_in):
    scaled = weight_grad * (codes.astype(jnp.float32) - 1.5) * fan_in ** (-0.5)
    return lax.optimization_barrier(jnp.sum(scaled.reshape(groups, -1, scaled.shape[1]), axis=1))

def norm_backward(hidden, inv_rms, gain_row, normed_cot, grad_out):
    hidden_f = hidden.astype(jnp.float32)
    scaled = gain_row * normed_cot
    total = grad_out.astype(jnp.float32) + inv_rms * scaled
    total = total - hidden_f * inv_rms ** 3 * lax.optimization_barrier(jnp.mean(scaled * hidden_f, axis=-1, keepdims=True))
    return total.astype(jnp.bfloat16)

def slot_index(routed):
    blocks = routed.reshape(N_EXPERT, TOK_DEV * TOP).astype(jnp.int32)
    onehot = (blocks[:, :, None] == jnp.arange(EXPERTS, dtype=jnp.int32)[None, None, :]).astype(jnp.int32)
    rank = lax.optimization_barrier(jnp.sum(onehot * (jnp.cumsum(onehot, axis=1) - 1), axis=-1))
    source = jnp.arange(N_EXPERT, dtype=jnp.int32)[:, None]
    return (blocks * RECV + source * MOST + rank).reshape(-1).astype(jnp.int32)

def reference(inputs, norm_gain, expert_ids, route_weights, gate_codes, up_codes, down_codes, gate_steps, up_steps, down_steps, out_grad):
    contract_rows = (((0,), (0,)), ((), ()))
    groups_d = D // GROUP
    groups_f = FF // GROUP
    saved_inputs = [[None] * MICRO for unused in range(LAYERS)]
    outputs_list = [[None] * MICRO for unused in range(LAYERS)]
    grads_list = [[None] * MICRO for unused in range(LAYERS)]
    gate_accum = [jnp.zeros((EXPERTS, groups_d, FF), jnp.float32) for unused in range(LAYERS)]
    up_accum = [jnp.zeros((EXPERTS, groups_d, FF), jnp.float32) for unused in range(LAYERS)]
    down_accum = [jnp.zeros((EXPERTS, groups_f, D), jnp.float32) for unused in range(LAYERS)]

    def run_forward(arrays):
        w_gate = dequant(arrays[1], arrays[4], D)
        w_up = dequant(arrays[2], arrays[5], D)
        w_down = dequant(arrays[3], arrays[6], FF)
        return expert_forward(arrays[0], w_gate, w_up, w_down)[0]

    def run_backward(arrays):
        w_gate = dequant(arrays[2], arrays[5], D)
        w_up = dequant(arrays[3], arrays[6], D)
        w_down = dequant(arrays[4], arrays[7], FF)
        gate_pre, up_pre = expert_gates(arrays[0], w_gate, w_up)
        row_grad, gate_cot, up_cot, activated = expert_backward(arrays[1], gate_pre, up_pre, w_gate, w_up, w_down)
        gate_part = step_grad(lax.dot_general(arrays[0], gate_cot, contract_rows, preferred_element_type=jnp.float32), arrays[2], groups_d, D)
        up_part = step_grad(lax.dot_general(arrays[0], up_cot, contract_rows, preferred_element_type=jnp.float32), arrays[3], groups_d, D)
        down_part = step_grad(lax.dot_general(activated, arrays[1], contract_rows, preferred_element_type=jnp.float32), arrays[4], groups_f, FF)
        return (row_grad, gate_part, up_part, down_part)
    for micro in range(MICRO):
        hidden = inputs[micro]
        for layer in range(LAYERS):
            saved_inputs[layer][micro] = hidden
            normed, inv_rms = normalize(hidden, norm_gain[layer])
            index = slot_index(expert_ids[layer, micro])
            buffer = jnp.zeros((EXPERTS * RECV, D), jnp.bfloat16).at[index].set(jnp.repeat(normed, TOP, axis=0))
            results = lax.map(run_forward, (buffer.reshape(EXPERTS, RECV, D), gate_codes[layer], up_codes[layer], down_codes[layer], gate_steps[layer], up_steps[layer], down_steps[layer]))
            gathered = results.reshape(EXPERTS * RECV, D)[index].reshape(TOKENS, TOP, D).astype(jnp.float32)
            mixed = lax.optimization_barrier(jnp.sum(route_weights[layer, micro][:, :, None] * gathered, axis=1))
            hidden = (hidden.astype(jnp.float32) + mixed).astype(jnp.bfloat16)
            outputs_list[layer][micro] = hidden
    for micro in range(MICRO):
        grad_out = out_grad[micro]
        for layer in range(LAYERS - 1, -1, -1):
            hidden = saved_inputs[layer][micro]
            normed, inv_rms = normalize(hidden, norm_gain[layer])
            index = slot_index(expert_ids[layer, micro])
            weights = route_weights[layer, micro]
            out_cot = (weights[:, :, None] * grad_out.astype(jnp.float32)[:, None, :]).astype(jnp.bfloat16)
            token_buffer = jnp.zeros((EXPERTS * RECV, D), jnp.bfloat16).at[index].set(jnp.repeat(normed, TOP, axis=0))
            cot_buffer = jnp.zeros((EXPERTS * RECV, D), jnp.bfloat16).at[index].set(out_cot.reshape(TOKENS * TOP, D))
            row_grads, gate_part, up_part, down_part = lax.map(run_backward, (token_buffer.reshape(EXPERTS, RECV, D), cot_buffer.reshape(EXPERTS, RECV, D), gate_codes[layer], up_codes[layer], down_codes[layer], gate_steps[layer], up_steps[layer], down_steps[layer]))
            returned = row_grads.reshape(EXPERTS * RECV, D)[index].reshape(TOKENS, TOP, D).astype(jnp.float32)
            normed_cot = lax.optimization_barrier(jnp.sum(returned, axis=1))
            grad_out = norm_backward(hidden, inv_rms, norm_gain[layer], normed_cot, grad_out)
            grads_list[layer][micro] = grad_out
            gate_accum[layer] = gate_accum[layer] + gate_part
            up_accum[layer] = up_accum[layer] + up_part
            down_accum[layer] = down_accum[layer] + down_part
    layer_outputs = jnp.stack([jnp.stack(outputs_list[layer]) for layer in range(LAYERS)])
    input_grads = jnp.stack([jnp.stack(grads_list[layer]) for layer in range(LAYERS)])
    return (layer_outputs, input_grads, jnp.stack(gate_accum), jnp.stack(up_accum), jnp.stack(down_accum))
```

```python
import functools

import jax
import jax.numpy as jnp
from jax import lax
from jax.experimental import pallas as pl
from jax.experimental.pallas import tpu as pltpu
from jax.sharding import PartitionSpec as P

MESH = pl.DeviceIdType.MESH
BF16 = jnp.bfloat16
F32 = jnp.float32

SECTIONS, NZ, NX, NC = 4, 8, 4, 2
EXPERTS = NZ * NX * NC
TOKENS, TOP, SLOTS = 32, 2, 2
WIDTH, HIDDEN, GROUP = 2048, 768, 64
PIECES, LANES = 8, 256
TILE = SLOTS * PIECES
CHAINS = 2
SOURCES = EXPERTS // CHAINS
ROWS = SOURCES * SLOTS

NT = (((1,), (1,)), ((), ()))
TN = (((0,), (0,)), ((), ()))


def dot(a, b, dims=(((1,), (0,)), ((), ()))):
    return lax.dot_general(a, b, dims, preferred_element_type=F32)


def iota(shape, dim):
    return lax.broadcasted_iota(jnp.int32, shape, dim)


def route_info(ids, weights):
    lane = iota((TOKENS, 128), 1)
    first, second = ids[:, 0:1], ids[:, 1:2]
    hot0 = (lane == first).astype(F32)
    hot1 = (lane == second).astype(F32)
    earlier = (iota((TOKENS, TOKENS), 1) < iota((TOKENS, TOKENS), 0)).astype(BF16)
    count = dot(earlier, (hot0 + hot1).astype(BF16))
    slot0 = first.astype(F32) * SLOTS + jnp.sum(hot0 * count, axis=1, keepdims=True)
    slot1 = second.astype(F32) * SLOTS + jnp.sum(hot1 * count, axis=1, keepdims=True)
    info = jnp.where(lane == 0, slot0, 0.0) + jnp.where(lane == 1, slot1, 0.0)
    info = info + jnp.where(lane == 2, weights[:, 0:1], 0.0)
    return info + jnp.where(lane == 3, weights[:, 1:2], 0.0)


def place_matrix(info, weighted):
    spread = (iota((TOKENS, TOKENS * PIECES), 1) // PIECES == iota((TOKENS, TOKENS * PIECES), 0)).astype(BF16)
    cols = dot(info.astype(BF16), spread, TN)
    shape = (EXPERTS * TILE, TOKENS * PIECES)
    piece = iota((1, TOKENS * PIECES), 1) % PIECES
    at0 = cols[0:1, :].astype(jnp.int32) * PIECES + piece
    at1 = cols[1:2, :].astype(jnp.int32) * PIECES + piece
    row = iota(shape, 0)
    w0, w1 = (cols[2:3, :], cols[3:4, :]) if weighted else (1.0, 1.0)
    return (jnp.where(row == at0, w0, 0.0) + jnp.where(row == at1, w1, 0.0)).astype(BF16)


def take_matrix(info, weighted):
    spread = (iota((TOKENS * PIECES, TOKENS), 0) // PIECES == iota((TOKENS * PIECES, TOKENS), 1)).astype(BF16)
    rows = dot(spread, info.astype(BF16))
    shape = (TOKENS * PIECES, EXPERTS * TILE)
    piece = iota((TOKENS * PIECES, 1), 0) % PIECES
    at0 = rows[:, 0:1].astype(jnp.int32) * PIECES + piece
    at1 = rows[:, 1:2].astype(jnp.int32) * PIECES + piece
    col = iota(shape, 1)
    w0, w1 = (rows[:, 2:3], rows[:, 3:4]) if weighted else (1.0, 1.0)
    return (jnp.where(col == at0, w0, 0.0) + jnp.where(col == at1, w1, 0.0)).astype(BF16)


def token_sum(values):
    shaped = values.reshape(TOKENS, PIECES, LANES)
    total = jnp.sum(jnp.sum(shaped, axis=2, keepdims=True), axis=1, keepdims=True)
    return jnp.broadcast_to(total, (TOKENS, PIECES, LANES)).reshape(TOKENS * PIECES, LANES)


def kernel(
    x_ref, gain_ref, ids_ref, wts_ref, gc_hbm, uc_hbm, dc_hbm, gs_ref, us_ref, ds_ref, og_ref,
    lo_ref, ig_ref, gg_ref, ug_ref, dg_ref,
    gcode, ucode, dcode, w_gu, w_d,
    f_recv, r_recv, b_recv, q_recv, send_f, send_b, r_send, q_send,
    place_a, place_b, take_w, take_1,
    h_in, h_out, g_in, g_out, info_own, info_next, info_prev, gain8,
    wide, home, x_rows, pre, act, cot, gu_cot,
    code_sem, f_sem, r_sem, b_sem, q_sem, far_sem, sent_f, sent_b, sent_r, sent_q, sent_far,
):
    s = lax.axis_index("section")
    e = lax.axis_index("expert")
    z, x, c = e // (NX * NC), (e // NC) % NX, e % NC
    first, last = s == 0, s == SECTIONS - 1

    def index_of(zz, xx, cc):
        return (zz * NX + xx) * NC + cc

    barrier = pltpu.get_barrier_semaphore()

    def greet(section):
        def one(k, carry):
            pl.semaphore_signal(barrier, inc=1, device_id=(section, lax.rem(e + k, EXPERTS)), device_id_type=MESH)
            return carry
        return one

    lax.fori_loop(1, EXPERTS, greet(s), 0)

    @pl.when(s > 0)
    def _():
        lax.fori_loop(0, EXPERTS, greet(s - 1), 0)

    @pl.when(s < SECTIONS - 1)
    def _():
        lax.fori_loop(0, EXPERTS, greet(s + 1), 0)

    loads = [
        pltpu.make_async_copy(gc_hbm, gcode, code_sem.at[0]),
        pltpu.make_async_copy(uc_hbm, ucode, code_sem.at[1]),
        pltpu.make_async_copy(dc_hbm, dcode, code_sem.at[2]),
    ]
    for load in loads:
        load.start()

    info_own[...] = route_info(ids_ref[...], wts_ref[...])
    for p in range(PIECES):
        gain8[p : p + 1, :] = gain_ref[0:1, p * LANES : (p + 1) * LANES]

    def to_pieces(source):
        for p in range(PIECES):
            part = source[:, p * LANES : (p + 1) * LANES].astype(F32)
            for half in range(2):
                home[half, pl.ds(p, TOKENS, stride=PIECES), :] = part[:, half * 128 : (half + 1) * 128]
        return jnp.concatenate([home[0], home[1]], axis=1)

    def from_pieces(values, out_ref):
        for half in range(2):
            home[half] = values[:, half * 128 : (half + 1) * 128]
        for p in range(PIECES):
            for half in range(2):
                lanes = pl.ds(p * LANES + half * 128, 128)
                out_ref[:, lanes] = home[half, pl.ds(p, TOKENS, stride=PIECES), :].astype(out_ref.dtype)

    def far_z(j):
        return lax.rem(z + jnp.where(j % 2 == 0, 4 + j // 2, 3 - j // 2), NZ)

    X_ORDER = (2, 1, 3, 0)

    def remote(src, dst, ssem, rsem, section, target):
        pltpu.make_async_remote_copy(
            src_ref=src, dst_ref=dst, send_sem=ssem, recv_sem=rsem, device_id=(section, target), device_id_type=MESH
        ).start()

    chain, order = c, z * NX + x

    def scatter(place, values, buffer, recv, rsem, ssem, section, own_plane):
        def plane(j, skip):
            zz = far_z(j)
            block = pl.ds(pl.multiple_of(zz * NX * NC * TILE, 128), NX * NC * TILE)
            packed = dot(place[block, :], values).astype(BF16)
            buffer[pl.ds(zz * NX * NC, NX * NC)] = packed.reshape(NX * NC, TILE, LANES)
            for dx in X_ORDER:
                for dc in (1, 0):
                    target = index_of(zz, lax.rem(x + dx, NX), lax.rem(c + dc, NC))
                    if skip and dx == 0 and dc == 0:
                        pltpu.make_async_copy(buffer.at[e], recv.at[chain, order], rsem.at[chain]).start()
                    else:
                        remote(buffer.at[target], recv.at[chain, order], ssem, rsem.at[chain], section, target)

        def loop(j, carry):
            plane(j, False)
            return carry

        lax.fori_loop(0, NZ - 1, loop, 0)
        plane(NZ - 1, own_plane)

    def give_back(ch, buffer, recv, rsem, ssem):
        def plane(j, own):
            zz = far_z(j)
            block = pl.ds(pl.multiple_of(zz * NX * TILE, 64), NX * TILE)
            rows = jnp.concatenate([wide[0, block, :], wide[1, block, :]], axis=1).astype(BF16)
            buffer[ch, pl.ds(zz * NX, NX)] = rows.reshape(NX, TILE, LANES)
            for dx in X_ORDER:
                xx = lax.rem(x + dx, NX)
                target = index_of(zz, xx, ch)
                src, dst = buffer.at[ch, zz * NX + xx], recv.at[e]
                if own and dx == 0:
                    @pl.when(ch == c)
                    def _():
                        pltpu.make_async_copy(src, dst, rsem).start()

                    @pl.when(ch != c)
                    def _():
                        remote(src, dst, ssem, rsem, s, target)
                else:
                    remote(src, dst, ssem, rsem, s, target)

        def loop(j, carry):
            plane(j, False)
            return carry

        lax.fori_loop(0, NZ - 1, loop, 0)
        plane(NZ - 1, True)

    def wait_all(ref, sem):
        pltpu.make_async_copy(ref, ref, sem).wait()

    own_info = info_own[...]

    @pl.when(first)
    def _():
        values = to_pieces(x_ref)
        h_in[...] = values.astype(BF16)
        place_b[...] = place_matrix(own_info, False)

    @pl.when(last)
    def _():
        values = to_pieces(og_ref)
        g_in[...] = values.astype(BF16)
        place_a[...] = place_matrix(own_info, True)

    neighbours = jnp.where(first, 0, 1) + jnp.where(last, 0, 1)
    pl.semaphore_wait(barrier, EXPERTS - 1 + neighbours * EXPERTS)

    @pl.when(first)
    def _():
        scatter(place_b, h_in[...], send_b, f_recv, f_sem, sent_b, 0, True)

    @pl.when(last)
    def _():
        scatter(place_a, g_in[...], send_f, b_recv, b_sem, sent_f, SECTIONS - 1, True)

    @pl.when(s > 0)
    def _():
        remote(info_own, info_next, sent_far.at[0], far_sem.at[0], s - 1, e)

    @pl.when(s < SECTIONS - 1)
    def _():
        remote(info_own, info_prev, sent_far.at[1], far_sem.at[1], s + 1, e)

    def dequant(code, steps, out, col, fan_in, groups):
        def one(g, carry):
            rows = pl.ds(pl.multiple_of(g * GROUP, GROUP), GROUP)
            scale = steps[pl.ds(g, 1), :] * fan_in ** (-0.5)
            width = code.shape[1]
            out[rows, col : col + width] = ((code[rows, :].astype(F32) - 1.5) * scale).astype(BF16)
            return carry
        lax.fori_loop(0, groups, one, 0)

    loads[0].wait()
    dequant(gcode, gs_ref, w_gu, 0, WIDTH, WIDTH // GROUP)
    loads[1].wait()
    dequant(ucode, us_ref, w_gu, HIDDEN, WIDTH, WIDTH // GROUP)
    loads[2].wait()
    dequant(dcode, ds_ref, w_d, 0, HIDDEN, HIDDEN // GROUP)

    take_w[...] = take_matrix(own_info, True)
    take_1[...] = take_matrix(own_info, False)

    @pl.when(s < SECTIONS - 1)
    def _():
        wait_all(info_next, far_sem.at[0])
        place_a[...] = place_matrix(info_next[...], False)

    @pl.when(s > 0)
    def _():
        wait_all(info_prev, far_sem.at[1])
        place_b[...] = place_matrix(info_prev[...], True)

    def spread_out(recv, ch):
        flat = recv[ch].reshape(SOURCES * TILE, LANES).astype(F32)
        for half in range(2):
            wide[half] = flat[:, half * 128 : (half + 1) * 128]
        return [
            jnp.concatenate([wide[half, pl.ds(p, ROWS, stride=PIECES), :] for half in range(2)], axis=1)
            for p in range(PIECES)
        ]

    def collect(p, part):
        for half in range(2):
            wide[half, pl.ds(p, ROWS, stride=PIECES), :] = part[:, half * 128 : (half + 1) * 128]

    def rows_of(ch):
        return pl.ds(pl.multiple_of(ch * ROWS, ROWS), ROWS)

    def gates(ch):
        wait_all(f_recv.at[ch], f_sem.at[ch])
        parts = spread_out(f_recv, ch)
        square = functools.reduce(lambda a, b: a + b, [jnp.sum(q * q, axis=1, keepdims=True) for q in parts])
        inv = lax.rsqrt(square * (1.0 / WIDTH) + 1e-06)
        rows = rows_of(ch)
        for p in range(PIECES):
            lanes = slice(p * LANES, (p + 1) * LANES)
            x_rows[rows, lanes] = (parts[p] * inv * gain_ref[0:1, lanes]).astype(BF16)
        pre[rows, :] = dot(x_rows[rows, :], w_gu[...])
        gate, up = pre[rows, :HIDDEN], pre[rows, HIDDEN:]
        act[rows, :] = (gate * jax.nn.sigmoid(gate) * up).astype(BF16)

    def down(ch):
        rows = rows_of(ch)
        for p in range(PIECES):
            collect(p, dot(act[rows, :], w_d[:, p * LANES : (p + 1) * LANES]))
        give_back(ch, r_send, r_recv, r_sem, sent_r)

    def backward(ch):
        wait_all(b_recv.at[ch], b_sem.at[ch])
        parts = spread_out(b_recv, ch)
        rows = rows_of(ch)
        for p in range(PIECES):
            cot[rows, p * LANES : (p + 1) * LANES] = parts[p].astype(BF16)
        act_cot = dot(cot[rows, :], w_d[...], NT)
        gate, up = pre[rows, :HIDDEN], pre[rows, HIDDEN:]
        sig = jax.nn.sigmoid(gate)
        gu_cot[rows, :HIDDEN] = (act_cot * up * sig * (1.0 + gate * (1.0 - sig))).astype(BF16)
        gu_cot[rows, HIDDEN:] = (act_cot * gate * sig).astype(BF16)
        for p in range(PIECES):
            collect(p, dot(gu_cot[rows, :], w_gu[p * LANES : (p + 1) * LANES, :], NT))
        give_back(ch, q_send, q_recv, q_sem, sent_q)

    def each_chain(step):
        def one(ch, carry):
            step(ch)
            return carry
        lax.fori_loop(0, CHAINS, one, 0)

    def home_forward():
        wait_all(r_recv, r_sem)
        mixed = dot(take_w[...], r_recv[...].reshape(EXPERTS * TILE, LANES))

        @pl.when(s > 0)
        def _():
            wait_all(h_in, far_sem.at[2])

        return (h_in[...].astype(F32) + mixed).astype(BF16)

    def home_backward():
        wait_all(q_recv, q_sem)
        normed_cot = dot(take_1[...], q_recv[...].reshape(EXPERTS * TILE, LANES))

        @pl.when(s < SECTIONS - 1)
        def _():
            wait_all(g_in, far_sem.at[3])

        hidden = h_in[...].astype(F32)
        inv = lax.rsqrt(token_sum(hidden * hidden) * (1.0 / WIDTH) + 1e-06)
        gain = jnp.broadcast_to(gain8[...].reshape(1, PIECES, LANES), (TOKENS, PIECES, LANES))
        scaled = gain.reshape(TOKENS * PIECES, LANES) * normed_cot
        mean = token_sum(scaled * hidden) * (1.0 / WIDTH)
        total = g_in[...].astype(F32) + inv * scaled - hidden * (inv * inv * inv) * mean
        return total.astype(BF16)

    def step_grads():
        def gate_up(i, carry):
            rows = pl.ds(pl.multiple_of(i * 256, 256), 256)
            for code, out, col in ((gcode, gg_ref, 0), (ucode, ug_ref, HIDDEN)):
                grad = dot(x_rows[:, rows], gu_cot[:, col : col + HIDDEN], TN)
                grad = grad * (code[rows, :].astype(F32) - 1.5)
                summed = jnp.sum(grad.reshape(256 // GROUP, GROUP, HIDDEN), axis=1) * WIDTH ** (-0.5)
                for g in range(256 // GROUP):
                    out[pl.ds(i * (256 // GROUP) + g, 1), :] = summed[g : g + 1, :]
            return carry

        lax.fori_loop(0, WIDTH // 256, gate_up, 0)

        def down_part(i, carry):
            rows = pl.ds(pl.multiple_of(i * 256, 256), 256)
            for col in range(0, WIDTH, 1024):
                grad = dot(act[:, rows], cot[:, col : col + 1024], TN)
                grad = grad * (dcode[rows, col : col + 1024].astype(F32) - 1.5)
                summed = jnp.sum(grad.reshape(256 // GROUP, GROUP, 1024), axis=1) * HIDDEN ** (-0.5)
                for g in range(256 // GROUP):
                    dg_ref[pl.ds(i * (256 // GROUP) + g, 1), col : col + 1024] = summed[g : g + 1, :]
            return carry

        lax.fori_loop(0, HIDDEN // 256, down_part, 0)

    @pl.when(s < SECTIONS - 1)
    def _():
        def forward(ch):
            gates(ch)
            down(ch)

        each_chain(forward)
        h_out[...] = home_forward()
        scatter(place_a, h_out[...], send_f, f_recv, f_sem, sent_f, s + 1, False)
        remote(h_out, h_in, sent_far.at[2], far_sem.at[2], s + 1, e)
        from_pieces(h_out[...].astype(F32), lo_ref)
        each_chain(backward)

    @pl.when(last)
    def _():
        def turn(ch):
            gates(ch)
            backward(ch)

        each_chain(turn)
        each_chain(down)
        h_out[...] = home_forward()
        from_pieces(h_out[...].astype(F32), lo_ref)

    @pl.when(first)
    def _():
        step_grads()

    g_out[...] = home_backward()

    @pl.when(s > 0)
    def _():
        scatter(place_b, g_out[...], send_b, b_recv, b_sem, sent_b, s - 1, False)
        remote(g_out, g_in, sent_far.at[3], far_sem.at[3], s - 1, e)

    from_pieces(g_out[...].astype(F32), ig_ref)

    @pl.when(s > 0)
    def _():
        step_grads()

    @pl.when(first)
    def _():
        wait_all(send_f, sent_f)
        wait_all(send_b.at[pl.ds(0, EXPERTS - 1)], sent_b)

    @pl.when(last)
    def _():
        wait_all(send_f.at[pl.ds(0, EXPERTS - 1)], sent_f)
        wait_all(send_b, sent_b)

    @pl.when(jnp.logical_and(s > 0, s < SECTIONS - 1))
    def _():
        wait_all(send_f, sent_f)
        wait_all(send_b, sent_b)

    wait_all(send_f.at[pl.ds(0, EXPERTS - 1)], sent_r)
    wait_all(send_f.at[pl.ds(0, EXPERTS - 1)], sent_q)

    @pl.when(s > 0)
    def _():
        wait_all(info_own, sent_far.at[0])
        wait_all(g_out, sent_far.at[3])

    @pl.when(s < SECTIONS - 1)
    def _():
        wait_all(info_own, sent_far.at[1])
        wait_all(h_out, sent_far.at[2])


def body(inputs, norm_gain, expert_ids, route_weights, gate_codes, up_codes, down_codes, gate_steps, up_steps, down_steps, out_grad):
    vmem = pl.BlockSpec(memory_space=pltpu.VMEM)
    hbm = pl.BlockSpec(memory_space=pl.ANY)
    message = (TILE, LANES)
    pieces = (TOKENS * PIECES, LANES)
    slots = EXPERTS * TILE
    both = CHAINS * ROWS
    scratch = [
        pltpu.VMEM((WIDTH, HIDDEN), BF16),
        pltpu.VMEM((WIDTH, HIDDEN), BF16),
        pltpu.VMEM((HIDDEN, WIDTH), BF16),
        pltpu.VMEM((WIDTH, 2 * HIDDEN), BF16),
        pltpu.VMEM((HIDDEN, WIDTH), BF16),
        pltpu.VMEM((CHAINS, SOURCES) + message, BF16),
        pltpu.VMEM((EXPERTS,) + message, BF16),
        pltpu.VMEM((CHAINS, SOURCES) + message, BF16),
        pltpu.VMEM((EXPERTS,) + message, BF16),
        pltpu.VMEM((EXPERTS,) + message, BF16),
        pltpu.VMEM((EXPERTS,) + message, BF16),
        pltpu.VMEM((CHAINS, SOURCES) + message, BF16),
        pltpu.VMEM((CHAINS, SOURCES) + message, BF16),
        pltpu.VMEM((slots, TOKENS * PIECES), BF16),
        pltpu.VMEM((slots, TOKENS * PIECES), BF16),
        pltpu.VMEM((TOKENS * PIECES, slots), BF16),
        pltpu.VMEM((TOKENS * PIECES, slots), BF16),
        pltpu.VMEM(pieces, BF16),
        pltpu.VMEM(pieces, BF16),
        pltpu.VMEM(pieces, BF16),
        pltpu.VMEM(pieces, BF16),
        pltpu.VMEM((TOKENS, 128), F32),
        pltpu.VMEM((TOKENS, 128), F32),
        pltpu.VMEM((TOKENS, 128), F32),
        pltpu.VMEM((PIECES, LANES), F32),
        pltpu.VMEM((2, SOURCES * TILE, 128), F32),
        pltpu.VMEM((2, TOKENS * PIECES, 128), F32),
        pltpu.VMEM((both, WIDTH), BF16),
        pltpu.VMEM((both, 2 * HIDDEN), F32),
        pltpu.VMEM((both, HIDDEN), BF16),
        pltpu.VMEM((both, WIDTH), BF16),
        pltpu.VMEM((both, 2 * HIDDEN), BF16),
        pltpu.SemaphoreType.DMA((3,)),
        pltpu.SemaphoreType.DMA((CHAINS,)),
        pltpu.SemaphoreType.DMA,
        pltpu.SemaphoreType.DMA((CHAINS,)),
        pltpu.SemaphoreType.DMA,
        pltpu.SemaphoreType.DMA((4,)),
        pltpu.SemaphoreType.DMA,
        pltpu.SemaphoreType.DMA,
        pltpu.SemaphoreType.DMA,
        pltpu.SemaphoreType.DMA,
        pltpu.SemaphoreType.DMA((4,)),
    ]
    outs = pl.pallas_call(
        kernel,
        out_shape=(
            jax.ShapeDtypeStruct((TOKENS, WIDTH), BF16),
            jax.ShapeDtypeStruct((TOKENS, WIDTH), BF16),
            jax.ShapeDtypeStruct((WIDTH // GROUP, HIDDEN), F32),
            jax.ShapeDtypeStruct((WIDTH // GROUP, HIDDEN), F32),
            jax.ShapeDtypeStruct((HIDDEN // GROUP, WIDTH), F32),
        ),
        in_specs=[vmem] * 4 + [hbm] * 3 + [vmem] * 4,
        out_specs=[vmem] * 5,
        scratch_shapes=scratch,
        compiler_params=pltpu.CompilerParams(
            collective_id=0, has_side_effects=True, vmem_limit_bytes=48 * 1024 * 1024
        ),
    )(
        inputs[0], norm_gain, expert_ids[0, 0], route_weights[0, 0],
        gate_codes[0, 0], up_codes[0, 0], down_codes[0, 0],
        gate_steps[0, 0], up_steps[0, 0], down_steps[0, 0], out_grad[0],
    )
    layer_out, input_grad, gate_grad, up_grad, down_grad = outs
    return (layer_out[None, None], input_grad[None, None], gate_grad[None, None], up_grad[None, None], down_grad[None, None])


def solution(mesh):
    in_specs = (
        P(None, "expert", None),
        P("section", None),
        P("section", None, "expert", None),
        P("section", None, "expert", None),
        P("section", "expert", None, None),
        P("section", "expert", None, None),
        P("section", "expert", None, None),
        P("section", "expert", None, None),
        P("section", "expert", None, None),
        P("section", "expert", None, None),
        P(None, "expert", None),
    )
    out_specs = (
        P("section", None, "expert", None),
        P("section", None, "expert", None),
        P("section", "expert", None, None),
        P("section", "expert", None, None),
        P("section", "expert", None, None),
    )
    return jax.shard_map(body, mesh=mesh, in_specs=in_specs, out_specs=out_specs, check_vma=False)
```

```python
import functools

import jax
import jax.numpy as jnp
from jax import lax
from jax.experimental import pallas as pl
from jax.experimental.pallas import tpu as pltpu
from jax.sharding import PartitionSpec as P

MESH = pl.DeviceIdType.MESH
BF16 = jnp.bfloat16
F32 = jnp.float32

SECTIONS, NZ, NX, NC = 4, 8, 4, 2
EXPERTS = NZ * NX * NC
TOKENS, TOP, SLOTS = 32, 2, 2
WIDTH, HIDDEN, GROUP = 2048, 768, 64
PIECES, LANES = 8, 256
TILE = SLOTS * PIECES
CHAINS = 2
SOURCES = EXPERTS // CHAINS
ROWS = SOURCES * SLOTS

NT = (((1,), (1,)), ((), ()))
TN = (((0,), (0,)), ((), ()))


def dot(a, b, dims=(((1,), (0,)), ((), ()))):
    return lax.dot_general(a, b, dims, preferred_element_type=F32)


def iota(shape, dim):
    return lax.broadcasted_iota(jnp.int32, shape, dim)


def route_info(ids, weights):
    lane = iota((TOKENS, 128), 1)
    same = iota((TOKENS, TOKENS), 0) == iota((TOKENS, TOKENS), 1)
    first, second = [jnp.sum(jnp.where(same, ids[k : k + 1, :], 0), axis=1, keepdims=True) for k in range(TOP)]
    weight0, weight1 = [jnp.sum(jnp.where(same, weights[k : k + 1, :], 0.0), axis=1, keepdims=True) for k in range(TOP)]
    hot0 = (lane == first).astype(F32)
    hot1 = (lane == second).astype(F32)
    earlier = (iota((TOKENS, TOKENS), 1) < iota((TOKENS, TOKENS), 0)).astype(BF16)
    count = dot(earlier, (hot0 + hot1).astype(BF16))
    slot0 = first.astype(F32) * SLOTS + jnp.sum(hot0 * count, axis=1, keepdims=True)
    slot1 = second.astype(F32) * SLOTS + jnp.sum(hot1 * count, axis=1, keepdims=True)
    info = jnp.where(lane == 0, slot0, 0.0) + jnp.where(lane == 1, slot1, 0.0)
    info = info + jnp.where(lane == 2, weight0, 0.0)
    return info + jnp.where(lane == 3, weight1, 0.0)


def place_matrix(info, weighted):
    spread = (iota((TOKENS, TOKENS * PIECES), 1) // PIECES == iota((TOKENS, TOKENS * PIECES), 0)).astype(BF16)
    cols = dot(info.astype(BF16), spread, TN)
    shape = (EXPERTS * TILE, TOKENS * PIECES)
    piece = iota((1, TOKENS * PIECES), 1) % PIECES
    at0 = cols[0:1, :].astype(jnp.int32) * PIECES + piece
    at1 = cols[1:2, :].astype(jnp.int32) * PIECES + piece
    row = iota(shape, 0)
    w0, w1 = (cols[2:3, :], cols[3:4, :]) if weighted else (1.0, 1.0)
    return (jnp.where(row == at0, w0, 0.0) + jnp.where(row == at1, w1, 0.0)).astype(BF16)


def take_matrix(info, weighted):
    spread = (iota((TOKENS * PIECES, TOKENS), 0) // PIECES == iota((TOKENS * PIECES, TOKENS), 1)).astype(BF16)
    rows = dot(spread, info.astype(BF16))
    shape = (TOKENS * PIECES, EXPERTS * TILE)
    piece = iota((TOKENS * PIECES, 1), 0) % PIECES
    at0 = rows[:, 0:1].astype(jnp.int32) * PIECES + piece
    at1 = rows[:, 1:2].astype(jnp.int32) * PIECES + piece
    col = iota(shape, 1)
    w0, w1 = (rows[:, 2:3], rows[:, 3:4]) if weighted else (1.0, 1.0)
    return (jnp.where(col == at0, w0, 0.0) + jnp.where(col == at1, w1, 0.0)).astype(BF16)


def token_sum(values):
    shaped = values.reshape(TOKENS, PIECES, LANES)
    total = jnp.sum(jnp.sum(shaped, axis=2, keepdims=True), axis=1, keepdims=True)
    return jnp.broadcast_to(total, (TOKENS, PIECES, LANES)).reshape(TOKENS * PIECES, LANES)


def home_plane(z, x):
    return lax.rem(z + x, SECTIONS)


def kernel(
    x_hbm, gain_hbm, ids_hbm, wts_hbm, gc_hbm, uc_hbm, dc_hbm, gs_hbm, us_hbm, ds_hbm, og_hbm,
    lo_ref, ig_ref, gg_ref, ug_ref, dg_ref,
    x_ref, og_ref, gain_ref, ids_ref, wts_ref, gs_ref, us_ref, ds_ref,
    gcode, ucode, dcode, w_gu, w_d,
    f_recv, r_recv, b_recv, q_recv, send_first, send_home, r_send, q_send,
    place_first, place_f, place_b, take_w, take_1, take_last,
    h_all, g_all, g_final, lo_buf, ig_buf, g1_buf, note_own, notes,
    wide, home, x_rows, pre, act, cot, gu_cot,
    load_sem, f_sem, r_sem, b_sem, q_sem, note_sem, lo_sem, ig_sem, g1_sem,
    sent_first, sent_home, sent_r, sent_q, sent_note, sent_lo, sent_ig, sent_g1, planes_sem,
):
    s = lax.axis_index("section")
    e = lax.axis_index("expert")
    z, x, c = e // (NX * NC), (e // NC) % NX, e % NC
    first, last = s == 0, s == SECTIONS - 1
    at_home = s == home_plane(z, x)

    def index_of(zz, xx, cc):
        return (zz * NX + xx) * NC + cc

    barrier = pltpu.get_barrier_semaphore()

    def greet(k, carry):
        pl.semaphore_signal(barrier, inc=1, device_id=(s, lax.rem(e + k, EXPERTS)), device_id_type=MESH)
        return carry

    lax.fori_loop(1, EXPERTS, greet, 0)
    for k in range(1, SECTIONS):
        pl.semaphore_signal(barrier, inc=1, device_id=(lax.rem(s + k, SECTIONS), e), device_id_type=MESH)

    pairs = [
        (ids_hbm, ids_ref), (wts_hbm, wts_ref), (x_hbm, x_ref), (gain_hbm, gain_ref), (og_hbm, og_ref),
        (gs_hbm, gs_ref), (gc_hbm, gcode), (us_hbm, us_ref), (uc_hbm, ucode), (ds_hbm, ds_ref), (dc_hbm, dcode),
    ]
    loads = [pltpu.make_async_copy(src, dst, load_sem.at[k]) for k, (src, dst) in enumerate(pairs)]
    for load in loads:
        load.start()

    def to_pieces(source):
        for p in range(PIECES):
            part = source[:, p * LANES : (p + 1) * LANES].astype(F32)
            for half in range(2):
                home[half, pl.ds(p, TOKENS, stride=PIECES), :] = part[:, half * 128 : (half + 1) * 128]
        return jnp.concatenate([home[0], home[1]], axis=1)

    def from_pieces(values, out_ref):
        for half in range(2):
            home[half] = values[:, half * 128 : (half + 1) * 128]
        for p in range(PIECES):
            for half in range(2):
                lanes = pl.ds(p * LANES + half * 128, 128)
                out_ref[:, lanes] = home[half, pl.ds(p, TOKENS, stride=PIECES), :].astype(out_ref.dtype)

    def far_z(j):
        return lax.rem(z + jnp.where(j % 2 == 0, 4 + j // 2, 3 - j // 2), NZ)

    def remote(src, dst, ssem, rsem, section, target):
        pltpu.make_async_remote_copy(
            src_ref=src, dst_ref=dst, send_sem=ssem, recv_sem=rsem, device_id=(section, target), device_id_type=MESH
        ).start()

    def send_or_copy(src, dst, ssem, rsem, section, target, own):
        @pl.when(own)
        def _():
            pltpu.make_async_copy(src, dst, rsem).start()

        @pl.when(jnp.logical_not(own))
        def _():
            remote(src, dst, ssem, rsem, section, target)

    def wait_all(ref, sem):
        pltpu.make_async_copy(ref, ref, sem).wait()

    chain, order = c, z * NX + x

    def scatter(place, values, buffer, recv, rsem, ssem, section):
        def pack(j):
            zz = far_z(j)
            block = pl.ds(pl.multiple_of(zz * NX * NC * TILE, 128), NX * NC * TILE)
            packed = dot(place[block, :], values).astype(BF16)
            buffer[pl.ds(zz * NX * NC, NX * NC)] = packed.reshape(NX * NC, TILE, LANES)

        def send(j, dx, dc):
            target = index_of(far_z(j), lax.rem(x + dx, NX), lax.rem(c + dc, NC))
            remote(buffer.at[target], recv.at[chain, order], ssem, rsem.at[chain], section, target)

        def farthest(j, carry):
            pack(j)
            send(j, 2, 1)
            send(j, 2, 0)
            return carry

        def middle(j, carry):
            for dx in (1, 3):
                send(j, dx, 1)
                send(j, dx, 0)
            return carry

        def line(j, carry):
            send(j, 0, 1)
            send(j, 0, 0)
            return carry

        lax.fori_loop(0, NZ, farthest, 0)
        lax.fori_loop(0, NZ, middle, 0)
        lax.fori_loop(0, NZ - 1, line, 0)
        send(NZ - 1, 0, 1)
        send_or_copy(buffer.at[e], recv.at[chain, order], ssem, rsem.at[chain], section, e, section == s)

    def give_back(ch, buffer, recv, rsem, ssem, in_plane):
        def unpack(j):
            zz = far_z(j)
            block = pl.ds(pl.multiple_of(zz * NX * TILE, 64), NX * TILE)
            rows = jnp.concatenate([wide[0, block, :], wide[1, block, :]], axis=1).astype(BF16)
            buffer[ch, pl.ds(zz * NX, NX)] = rows.reshape(NX, TILE, LANES)

        def place_of(j, dx):
            zz, xx = far_z(j), lax.rem(x + dx, NX)
            section = jnp.where(in_plane, s, home_plane(zz, xx))
            return buffer.at[ch, zz * NX + xx], section, index_of(zz, xx, ch)

        def send(j, dx):
            src, section, target = place_of(j, dx)
            remote(src, recv.at[e], ssem, rsem, section, target)

        def farthest(j, carry):
            unpack(j)
            send(j, 2)
            return carry

        def middle(j, carry):
            send(j, 1)
            send(j, 3)
            return carry

        def line(j, carry):
            send(j, 0)
            return carry

        lax.fori_loop(0, NZ, farthest, 0)
        lax.fori_loop(0, NZ, middle, 0)
        lax.fori_loop(0, NZ - 1, line, 0)
        src, section, target = place_of(NZ - 1, 0)
        send_or_copy(src, recv.at[e], ssem, rsem, section, target, jnp.logical_and(section == s, ch == c))

    loads[0].wait()
    loads[1].wait()
    loads[2].wait()
    loads[3].wait()
    loads[4].wait()
    note_own[0:TOKENS, 0:128] = route_info(ids_ref[...], wts_ref[...])
    note_own[0:TOKENS, 128:] = jnp.zeros((TOKENS, LANES - 128), F32)
    for p in range(PIECES):
        note_own[TOKENS + p : TOKENS + p + 1, :] = gain_ref[0:1, p * LANES : (p + 1) * LANES]
    own_info = note_own[0:TOKENS, 0:128]

    h_all[0] = to_pieces(x_ref).astype(BF16)

    @pl.when(first)
    def _():
        place_first[...] = place_matrix(own_info, False)

    g_all[SECTIONS] = to_pieces(og_ref).astype(BF16)

    @pl.when(last)
    def _():
        place_first[...] = place_matrix(own_info, True)

    pl.semaphore_wait(barrier, EXPERTS - 1 + SECTIONS - 1)

    def begin():
        scatter(place_first, h_all[0], send_first, f_recv, f_sem, sent_first, 0)

    @pl.when(jnp.logical_and(first, c == 0))
    def _():
        begin()

    @pl.when(last)
    def _():
        scatter(place_first, g_all[SECTIONS], send_first, b_recv, b_sem, sent_first, SECTIONS - 1)

    for k in range(1, SECTIONS):
        pl.semaphore_signal(planes_sem, inc=1, device_id=(lax.rem(s + k, SECTIONS), e), device_id_type=MESH)

    @pl.when(at_home)
    def _():
        notes[s] = note_own[...]

    @pl.when(jnp.logical_not(at_home))
    def _():
        remote(note_own, notes.at[s], sent_note, note_sem, home_plane(z, x), e)

    def dequant(code, steps, out, col, fan_in, groups):
        def one(g, carry):
            rows = pl.ds(pl.multiple_of(g * GROUP, GROUP), GROUP)
            scale = (steps[g] if len(steps.shape) == 3 else steps[pl.ds(g, 1), :]) * fan_in ** (-0.5)
            width = code.shape[1]
            out[rows, col : col + width] = ((code[rows, :].astype(F32) - 1.5) * scale).astype(BF16)
            return carry
        lax.fori_loop(0, groups, one, 0)

    loads[5].wait()
    loads[6].wait()
    dequant(gcode, gs_ref, w_gu, 0, WIDTH, WIDTH // GROUP)
    loads[7].wait()
    loads[8].wait()
    dequant(ucode, us_ref, w_gu, HIDDEN, WIDTH, WIDTH // GROUP)
    loads[9].wait()
    loads[10].wait()
    dequant(dcode, ds_ref, w_d, 0, HIDDEN, HIDDEN // GROUP)

    @pl.when(jnp.logical_and(first, c == 1))
    def _():
        begin()

    def info_of(layer):
        return notes[layer, 0:TOKENS, 0:128]

    pl.semaphore_wait(planes_sem, SECTIONS - 1)

    @pl.when(at_home)
    def _():
        wait_all(notes.at[pl.ds(0, SECTIONS - 1)], note_sem)
        take_w[0] = take_matrix(info_of(0), True)
        place_f[0] = place_matrix(info_of(1), False)

    def spread_out(recv, ch):
        flat = recv[ch].reshape(SOURCES * TILE, LANES).astype(F32)
        for half in range(2):
            wide[half] = flat[:, half * 128 : (half + 1) * 128]
        return [
            jnp.concatenate([wide[half, pl.ds(p, ROWS, stride=PIECES), :] for half in range(2)], axis=1)
            for p in range(PIECES)
        ]

    def collect(p, part):
        for half in range(2):
            wide[half, pl.ds(p, ROWS, stride=PIECES), :] = part[:, half * 128 : (half + 1) * 128]

    def rows_of(ch):
        return pl.ds(pl.multiple_of(ch * ROWS, ROWS), ROWS)

    def gates(ch):
        wait_all(f_recv.at[ch], f_sem.at[ch])
        parts = spread_out(f_recv, ch)
        square = functools.reduce(lambda a, b: a + b, [jnp.sum(q * q, axis=1, keepdims=True) for q in parts])
        inv = lax.rsqrt(square * (1.0 / WIDTH) + 1e-06)
        rows = rows_of(ch)
        for p in range(PIECES):
            lanes = slice(p * LANES, (p + 1) * LANES)
            x_rows[rows, lanes] = (parts[p] * inv * gain_ref[0:1, lanes]).astype(BF16)
        pre[rows, :] = dot(x_rows[rows, :], w_gu[...])
        gate, up = pre[rows, :HIDDEN], pre[rows, HIDDEN:]
        act[rows, :] = (gate * jax.nn.sigmoid(gate) * up).astype(BF16)

    def down(ch):
        rows = rows_of(ch)
        for p in range(PIECES):
            collect(p, dot(act[rows, :], w_d[:, p * LANES : (p + 1) * LANES]))
        give_back(ch, r_send, r_recv, r_sem, sent_r, False)

    def backward(ch):
        wait_all(b_recv.at[ch], b_sem.at[ch])
        parts = spread_out(b_recv, ch)
        rows = rows_of(ch)
        for p in range(PIECES):
            cot[rows, p * LANES : (p + 1) * LANES] = parts[p].astype(BF16)
        act_cot = dot(cot[rows, :], w_d[...], NT)
        gate, up = pre[rows, :HIDDEN], pre[rows, HIDDEN:]
        sig = jax.nn.sigmoid(gate)
        gu_cot[rows, :HIDDEN] = (act_cot * up * sig * (1.0 + gate * (1.0 - sig))).astype(BF16)
        gu_cot[rows, HIDDEN:] = (act_cot * gate * sig).astype(BF16)
        for p in range(PIECES):
            collect(p, dot(gu_cot[rows, :], w_gu[p * LANES : (p + 1) * LANES, :], NT))
        give_back(ch, q_send, q_recv, q_sem, sent_q, first)

    def home_forward(layer):
        wait_all(r_recv, r_sem)
        mixed = dot(take_w[layer], r_recv[...].reshape(EXPERTS * TILE, LANES))
        h_all[layer + 1] = (h_all[layer].astype(F32) + mixed).astype(BF16)

    def hand_output(layer):
        send_or_copy(h_all.at[layer + 1], lo_buf, sent_lo, lo_sem, layer, e, s == layer)

    def norm_back(matrix, hidden, gain8, above):
        wait_all(q_recv, q_sem)
        normed_cot = dot(matrix, q_recv[...].reshape(EXPERTS * TILE, LANES))
        hidden = hidden.astype(F32)
        inv = lax.rsqrt(token_sum(hidden * hidden) * (1.0 / WIDTH) + 1e-06)
        gain = jnp.broadcast_to(gain8.reshape(1, PIECES, LANES), (TOKENS, PIECES, LANES))
        scaled = gain.reshape(TOKENS * PIECES, LANES) * normed_cot
        mean = token_sum(scaled * hidden) * (1.0 / WIDTH)
        total = above.astype(F32) + inv * scaled - hidden * (inv * inv * inv) * mean
        return total.astype(BF16)

    def home_backward(layer):
        gain8 = notes[layer, TOKENS : TOKENS + PIECES, :]
        g_all[layer] = norm_back(take_1[layer - 1], h_all[layer], gain8, g_all[layer + 1])
        k = SECTIONS - 2 + layer
        scatter(place_b.at[layer - 1], g_all[layer], send_home.at[k], b_recv, b_sem, sent_home.at[k], layer - 1)
        send_or_copy(g_all.at[layer], ig_buf, sent_ig, ig_sem, layer, e, s == layer)

        @pl.when(layer == 1)
        def _():
            send_or_copy(g_all.at[layer], g1_buf, sent_g1, g1_sem, 0, e, s == 0)

        @pl.when(layer > 1)
        def _():
            prepare_back(layer - 1)

    def prepare_back(layer):
        take_1[layer - 1] = take_matrix(info_of(layer), False)
        place_b[layer - 1] = place_matrix(info_of(layer - 1), True)

    def step_grads():
        def gate_up(i, carry):
            rows = pl.ds(pl.multiple_of(i * 256, 256), 256)
            for code, out, col in ((gcode, gg_ref, 0), (ucode, ug_ref, HIDDEN)):
                grad = dot(x_rows[:, rows], gu_cot[:, col : col + HIDDEN], TN)
                grad = grad * (code[rows, :].astype(F32) - 1.5)
                summed = jnp.sum(grad.reshape(256 // GROUP, GROUP, HIDDEN), axis=1) * WIDTH ** (-0.5)
                for g in range(256 // GROUP):
                    out[pl.ds(i * (256 // GROUP) + g, 1), :] = summed[g : g + 1, :]
            return carry

        lax.fori_loop(0, WIDTH // 256, gate_up, 0)

        def down_part(i, carry):
            rows = pl.ds(pl.multiple_of(i * 256, 256), 256)
            for col in range(0, WIDTH, 1024):
                grad = dot(act[:, rows], cot[:, col : col + 1024], TN)
                grad = grad * (dcode[rows, col : col + 1024].astype(F32) - 1.5)
                summed = jnp.sum(grad.reshape(256 // GROUP, GROUP, 1024), axis=1) * HIDDEN ** (-0.5)
                for g in range(256 // GROUP):
                    dg_ref[i * (256 // GROUP) + g, :, col : col + 1024] = summed[g : g + 1, :]
            return carry

        lax.fori_loop(0, HIDDEN // 256, down_part, 0)

    def forward_layer(layer, carry):
        @pl.when(s == layer)
        def _():
            def expert(ch, carry):
                gates(ch)
                down(ch)
                return carry

            lax.fori_loop(0, CHAINS, expert, 0)

        @pl.when(at_home)
        def _():
            home_forward(layer)
            scatter(
                place_f.at[layer], h_all[layer + 1], send_home.at[layer], f_recv, f_sem, sent_home.at[layer], layer + 1
            )
            hand_output(layer)
            take_w[layer + 1] = take_matrix(info_of(layer + 1), True)

            @pl.when(layer < SECTIONS - 2)
            def _():
                place_f[layer + 1] = place_matrix(info_of(layer + 2), False)

            @pl.when(layer == SECTIONS - 2)
            def _():
                prepare_back(SECTIONS - 1)

        return carry

    lax.fori_loop(0, SECTIONS - 1, forward_layer, 0)

    @pl.when(first)
    def _():
        take_last[...] = take_matrix(own_info, False)

    def backward_layer(t, carry):
        layer = SECTIONS - 1 - t

        @pl.when(s == layer)
        def _():
            def expert(ch, carry):
                @pl.when(last)
                def _():
                    gates(ch)

                backward(ch)
                return carry

            lax.fori_loop(0, CHAINS, expert, 0)

        @pl.when(jnp.logical_and(at_home, layer > 0))
        def _():
            home_backward(layer)

        @pl.when(jnp.logical_and(last, layer == SECTIONS - 1))
        def _():
            def give(ch, carry):
                down(ch)
                return carry

            lax.fori_loop(0, CHAINS, give, 0)

        @pl.when(s == layer)
        def _():
            step_grads()

        @pl.when(jnp.logical_and(at_home, t == 1))
        def _():
            home_forward(SECTIONS - 1)
            hand_output(SECTIONS - 1)

        return carry

    lax.fori_loop(0, SECTIONS, backward_layer, 0)

    wait_all(lo_buf, lo_sem)
    from_pieces(lo_buf[...].astype(F32), lo_ref)

    @pl.when(first)
    def _():
        wait_all(g1_buf, g1_sem)
        gain8 = note_own[TOKENS : TOKENS + PIECES, :]
        g_final[...] = norm_back(take_last[...], h_all[0], gain8, g1_buf[...])
        from_pieces(g_final[...].astype(F32), ig_ref)

    @pl.when(s > 0)
    def _():
        wait_all(ig_buf, ig_sem)
        from_pieces(ig_buf[...].astype(F32), ig_ref)

    def wait_messages(sem, some, own):
        @pl.when(own)
        def _():
            wait_all(some.at[pl.ds(0, EXPERTS - 1)], sem)

        @pl.when(jnp.logical_not(own))
        def _():
            wait_all(some, sem)

    @pl.when(jnp.logical_or(first, last))
    def _():
        wait_all(send_first.at[pl.ds(0, EXPERTS - 1)], sent_first)

    wait_messages(sent_r, send_first, at_home)
    wait_messages(sent_q, send_first, jnp.logical_or(at_home, first))

    @pl.when(jnp.logical_not(at_home))
    def _():
        wait_all(note_own, sent_note)

    @pl.when(at_home)
    def _():
        for layer in range(SECTIONS - 1):
            wait_messages(sent_home.at[layer], send_first, s == layer + 1)
            wait_messages(sent_home.at[SECTIONS - 1 + layer], send_first, s == layer)
        wait_all(h_all.at[pl.ds(0, SECTIONS - 1)], sent_lo)

        @pl.when(first)
        def _():
            wait_all(g_all.at[pl.ds(0, SECTIONS - 1)], sent_ig)

        @pl.when(s > 0)
        def _():
            wait_all(g_all.at[pl.ds(0, SECTIONS - 2)], sent_ig)
            wait_all(g1_buf, sent_g1)


def give_out(*refs):
    count = len(refs) // 3
    taken, given, held, sems = refs[:count], refs[count : 2 * count], refs[2 * count : 3 * count], refs[-1]
    loads = [pltpu.make_async_copy(taken[k], held[k], sems.at[0, k]) for k in range(count)]
    stores = [pltpu.make_async_copy(held[k], given[k], sems.at[1, k]) for k in range(count)]
    for load in loads:
        load.start()
    for load, store in zip(loads, stores):
        load.wait()
        store.start()
    for store in stores:
        store.wait()


def body(inputs, norm_gain, expert_ids, route_weights, gate_codes, up_codes, down_codes, gate_steps, up_steps, down_steps, out_grad):
    vmem = pl.BlockSpec(memory_space=pltpu.VMEM)
    hbm = pl.BlockSpec(memory_space=pl.ANY)
    message = (TILE, LANES)
    pieces = (TOKENS * PIECES, LANES)
    slots = EXPERTS * TILE
    both = CHAINS * ROWS
    steps = SECTIONS - 1
    tokens = (TOKENS, WIDTH)
    gate_shape, down_shape = (WIDTH, HIDDEN), (HIDDEN, WIDTH)
    gate_steps_shape, down_steps_shape = (WIDTH // GROUP, HIDDEN), (HIDDEN // GROUP, WIDTH)
    place, take = (slots, TOKENS * PIECES), (TOKENS * PIECES, slots)
    dma = pltpu.SemaphoreType.DMA
    scratch = [
        pltpu.VMEM(tokens, BF16),
        pltpu.VMEM(tokens, BF16),
        pltpu.VMEM((1, WIDTH), F32),
        pltpu.VMEM((TOP, TOKENS), jnp.int32),
        pltpu.VMEM((TOP, TOKENS), F32),
        pltpu.VMEM(gate_steps_shape, F32),
        pltpu.VMEM(gate_steps_shape, F32),
        pltpu.VMEM((HIDDEN // GROUP, 1, WIDTH), F32),
        pltpu.VMEM(gate_shape, BF16),
        pltpu.VMEM(gate_shape, BF16),
        pltpu.VMEM(down_shape, BF16),
        pltpu.VMEM((WIDTH, 2 * HIDDEN), BF16),
        pltpu.VMEM(down_shape, BF16),
        pltpu.VMEM((CHAINS, SOURCES) + message, BF16),
        pltpu.VMEM((EXPERTS,) + message, BF16),
        pltpu.VMEM((CHAINS, SOURCES) + message, BF16),
        pltpu.VMEM((EXPERTS,) + message, BF16),
        pltpu.VMEM((EXPERTS,) + message, BF16),
        pltpu.VMEM((2 * steps, EXPERTS) + message, BF16),
        pltpu.VMEM((CHAINS, SOURCES) + message, BF16),
        pltpu.VMEM((CHAINS, SOURCES) + message, BF16),
        pltpu.VMEM(place, BF16),
        pltpu.VMEM((steps,) + place, BF16),
        pltpu.VMEM((steps,) + place, BF16),
        pltpu.VMEM((SECTIONS,) + take, BF16),
        pltpu.VMEM((steps,) + take, BF16),
        pltpu.VMEM(take, BF16),
        pltpu.VMEM((SECTIONS + 1,) + pieces, BF16),
        pltpu.VMEM((SECTIONS + 1,) + pieces, BF16),
        pltpu.VMEM(pieces, BF16),
        pltpu.VMEM(pieces, BF16),
        pltpu.VMEM(pieces, BF16),
        pltpu.VMEM(pieces, BF16),
        pltpu.VMEM((TOKENS + PIECES, LANES), F32),
        pltpu.VMEM((SECTIONS, TOKENS + PIECES, LANES), F32),
        pltpu.VMEM((2, SOURCES * TILE, 128), F32),
        pltpu.VMEM((2, TOKENS * PIECES, 128), F32),
        pltpu.VMEM((both, WIDTH), BF16),
        pltpu.VMEM((both, 2 * HIDDEN), F32),
        pltpu.VMEM((both, HIDDEN), BF16),
        pltpu.VMEM((both, WIDTH), BF16),
        pltpu.VMEM((both, 2 * HIDDEN), BF16),
        dma((11,)),
        dma((CHAINS,)),
        dma,
        dma((CHAINS,)),
        dma,
        dma,
        dma,
        dma,
        dma,
        dma,
        dma((2 * steps,)),
        dma,
        dma,
        dma,
        dma,
        dma,
        dma,
        pltpu.SemaphoreType.REGULAR,
    ]
    outs = pl.pallas_call(
        kernel,
        out_shape=(
            jax.ShapeDtypeStruct(tokens, BF16),
            jax.ShapeDtypeStruct(tokens, BF16),
            jax.ShapeDtypeStruct(gate_steps_shape, F32),
            jax.ShapeDtypeStruct(gate_steps_shape, F32),
            jax.ShapeDtypeStruct((HIDDEN // GROUP, 1, WIDTH), F32),
        ),
        in_specs=[hbm] * 11,
        out_specs=[vmem] * 5,
        scratch_shapes=scratch,
        compiler_params=pltpu.CompilerParams(
            collective_id=0, has_side_effects=True, vmem_limit_bytes=58 * 1024 * 1024
        ),
    )(
        inputs[0], norm_gain, jnp.transpose(expert_ids[0, 0]), jnp.transpose(route_weights[0, 0]),
        gate_codes[0, 0], up_codes[0, 0], down_codes[0, 0],
        gate_steps[0, 0], up_steps[0, 0], jnp.transpose(down_steps[0], (1, 0, 2)), out_grad[0],
    )
    layer_out, input_grad, gate_grad, up_grad, down_grad = pl.pallas_call(
        give_out,
        out_shape=tuple(jax.ShapeDtypeStruct(out.shape, out.dtype) for out in outs),
        in_specs=[hbm] * len(outs),
        out_specs=[hbm] * len(outs),
        scratch_shapes=[pltpu.VMEM(out.shape, out.dtype) for out in outs] + [dma((2, len(outs)))],
    )(*outs)
    return (layer_out[None, None], input_grad[None, None], gate_grad[None, None], up_grad[None, None], jnp.transpose(down_grad, (1, 0, 2))[None])


def solution(mesh):
    in_specs = (
        P(None, "expert", None),
        P("section", None),
        P("section", None, "expert", None),
        P("section", None, "expert", None),
        P("section", "expert", None, None),
        P("section", "expert", None, None),
        P("section", "expert", None, None),
        P("section", "expert", None, None),
        P("section", "expert", None, None),
        P("section", "expert", None, None),
        P(None, "expert", None),
    )
    out_specs = (
        P("section", None, "expert", None),
        P("section", None, "expert", None),
        P("section", "expert", None, None),
        P("section", "expert", None, None),
        P("section", "expert", None, None),
    )
    return jax.shard_map(body, mesh=mesh, in_specs=in_specs, out_specs=out_specs, check_vma=False)
```

```python
import functools

import jax
import jax.numpy as jnp
from jax import lax
from jax.experimental import pallas as pl
from jax.experimental.pallas import tpu as pltpu
from jax.sharding import PartitionSpec as P

MESH = pl.DeviceIdType.MESH
BF16 = jnp.bfloat16
F32 = jnp.float32

SECTIONS, NZ, NX, NC = 4, 8, 4, 2
EXPERTS = NZ * NX * NC
TOKENS, TOP, SLOTS = 32, 2, 2
WIDTH, HIDDEN, GROUP = 2048, 768, 64
PIECES, LANES = 8, 256
TILE = SLOTS * PIECES
CHAINS = 2
SOURCES = EXPERTS // CHAINS
ROWS = SOURCES * SLOTS

NT = (((1,), (1,)), ((), ()))
TN = (((0,), (0,)), ((), ()))


def dot(a, b, dims=(((1,), (0,)), ((), ()))):
    return lax.dot_general(a, b, dims, preferred_element_type=F32)


def iota(shape, dim):
    return lax.broadcasted_iota(jnp.int32, shape, dim)


def route_info(ids, weights):
    lane = iota((TOKENS, 128), 1)
    same = iota((TOKENS, TOKENS), 0) == iota((TOKENS, TOKENS), 1)
    first, second = [jnp.sum(jnp.where(same, ids[k : k + 1, :], 0), axis=1, keepdims=True) for k in range(TOP)]
    weight0, weight1 = [jnp.sum(jnp.where(same, weights[k : k + 1, :], 0.0), axis=1, keepdims=True) for k in range(TOP)]
    hot0 = (lane == first).astype(F32)
    hot1 = (lane == second).astype(F32)
    earlier = (iota((TOKENS, TOKENS), 1) < iota((TOKENS, TOKENS), 0)).astype(BF16)
    count = dot(earlier, (hot0 + hot1).astype(BF16))
    slot0 = first.astype(F32) * SLOTS + jnp.sum(hot0 * count, axis=1, keepdims=True)
    slot1 = second.astype(F32) * SLOTS + jnp.sum(hot1 * count, axis=1, keepdims=True)
    info = jnp.where(lane == 0, slot0, 0.0) + jnp.where(lane == 1, slot1, 0.0)
    info = info + jnp.where(lane == 2, weight0, 0.0)
    return info + jnp.where(lane == 3, weight1, 0.0)


def place_matrix(info, weighted):
    spread = (iota((TOKENS, TOKENS * PIECES), 1) // PIECES == iota((TOKENS, TOKENS * PIECES), 0)).astype(BF16)
    cols = dot(info.astype(BF16), spread, TN)
    shape = (EXPERTS * TILE, TOKENS * PIECES)
    piece = iota((1, TOKENS * PIECES), 1) % PIECES
    at0 = cols[0:1, :].astype(jnp.int32) * PIECES + piece
    at1 = cols[1:2, :].astype(jnp.int32) * PIECES + piece
    row = iota(shape, 0)
    w0, w1 = (cols[2:3, :], cols[3:4, :]) if weighted else (1.0, 1.0)
    return (jnp.where(row == at0, w0, 0.0) + jnp.where(row == at1, w1, 0.0)).astype(BF16)


def take_matrix(info, weighted):
    spread = (iota((TOKENS * PIECES, TOKENS), 0) // PIECES == iota((TOKENS * PIECES, TOKENS), 1)).astype(BF16)
    rows = dot(spread, info.astype(BF16))
    shape = (TOKENS * PIECES, EXPERTS * TILE)
    piece = iota((TOKENS * PIECES, 1), 0) % PIECES
    at0 = rows[:, 0:1].astype(jnp.int32) * PIECES + piece
    at1 = rows[:, 1:2].astype(jnp.int32) * PIECES + piece
    col = iota(shape, 1)
    w0, w1 = (rows[:, 2:3], rows[:, 3:4]) if weighted else (1.0, 1.0)
    return (jnp.where(col == at0, w0, 0.0) + jnp.where(col == at1, w1, 0.0)).astype(BF16)


def token_sum(values):
    shaped = values.reshape(TOKENS, PIECES, LANES)
    total = jnp.sum(jnp.sum(shaped, axis=2, keepdims=True), axis=1, keepdims=True)
    return jnp.broadcast_to(total, (TOKENS, PIECES, LANES)).reshape(TOKENS * PIECES, LANES)


def home_plane(z, x):
    return lax.rem(z + x, SECTIONS)


def kernel(
    x_hbm, gain_hbm, ids_hbm, wts_hbm, gc_hbm, uc_hbm, dc_hbm, gs_hbm, us_hbm, ds_hbm, og_hbm,
    lo_ref, ig_ref, gg_ref, ug_ref, dg_ref,
    x_ref, og_ref, gain_ref, ids_ref, wts_ref, gs_ref, us_ref, ds_ref,
    gcode, ucode, dcode, w_gu, w_d,
    f_recv, r_recv, b_recv, q_recv, send_first, send_home, r_send, q_send, relay_send, relay_recv,
    place_first, place_f, place_b, take_w, take_1, take_last,
    h_all, g_all, g_final, lo_buf, ig_buf, g1_buf, note_own, notes,
    wide, home, x_rows, pre, act, cot, gu_cot,
    load_sem, f_sem, r_sem, b_sem, q_sem, note_sem, lo_sem, ig_sem, g1_sem,
    sent_first, sent_home, sent_r, sent_q, sent_note, sent_lo, sent_ig, sent_g1, planes_sem, relay_sem, sent_relay, sent_on,
):
    s = lax.axis_index("section")
    e = lax.axis_index("expert")
    z, x, c = e // (NX * NC), (e // NC) % NX, e % NC
    first, last = s == 0, s == SECTIONS - 1
    at_home = s == home_plane(z, x)

    def index_of(zz, xx, cc):
        return (zz * NX + xx) * NC + cc

    barrier = pltpu.get_barrier_semaphore()

    def greet(k, carry):
        pl.semaphore_signal(barrier, inc=1, device_id=(s, lax.rem(e + k, EXPERTS)), device_id_type=MESH)
        return carry

    lax.fori_loop(1, EXPERTS, greet, 0)
    for k in range(1, SECTIONS):
        pl.semaphore_signal(barrier, inc=1, device_id=(lax.rem(s + k, SECTIONS), e), device_id_type=MESH)

    pairs = [
        (ids_hbm, ids_ref), (wts_hbm, wts_ref), (x_hbm, x_ref), (gain_hbm, gain_ref), (og_hbm, og_ref),
        (gs_hbm, gs_ref), (gc_hbm, gcode), (us_hbm, us_ref), (uc_hbm, ucode), (ds_hbm, ds_ref), (dc_hbm, dcode),
    ]
    loads = [pltpu.make_async_copy(src, dst, load_sem.at[k]) for k, (src, dst) in enumerate(pairs)]
    for load in loads:
        load.start()

    def to_pieces(source):
        for p in range(PIECES):
            part = source[:, p * LANES : (p + 1) * LANES].astype(F32)
            for half in range(2):
                home[half, pl.ds(p, TOKENS, stride=PIECES), :] = part[:, half * 128 : (half + 1) * 128]
        return jnp.concatenate([home[0], home[1]], axis=1)

    def from_pieces(values, out_ref):
        for half in range(2):
            home[half] = values[:, half * 128 : (half + 1) * 128]
        for p in range(PIECES):
            for half in range(2):
                lanes = pl.ds(p * LANES + half * 128, 128)
                out_ref[:, lanes] = home[half, pl.ds(p, TOKENS, stride=PIECES), :].astype(out_ref.dtype)

    def far_z(j):
        return lax.rem(z + jnp.where(j % 2 == 0, 4 + j // 2, 3 - j // 2), NZ)

    def remote(src, dst, ssem, rsem, section, target):
        pltpu.make_async_remote_copy(
            src_ref=src, dst_ref=dst, send_sem=ssem, recv_sem=rsem, device_id=(section, target), device_id_type=MESH
        ).start()

    def send_or_copy(src, dst, ssem, rsem, section, target, own):
        @pl.when(own)
        def _():
            pltpu.make_async_copy(src, dst, rsem).start()

        @pl.when(jnp.logical_not(own))
        def _():
            remote(src, dst, ssem, rsem, section, target)

    def wait_all(ref, sem):
        pltpu.make_async_copy(ref, ref, sem).wait()

    chain, order = c, z * NX + x

    def scatter(place, values, buffer, recv, rsem, ssem, section):
        def pack(j):
            zz = far_z(j)
            block = pl.ds(pl.multiple_of(zz * NX * NC * TILE, 128), NX * NC * TILE)
            packed = dot(place[block, :], values).astype(BF16)
            buffer[pl.ds(zz * NX * NC, NX * NC)] = packed.reshape(NX * NC, TILE, LANES)

        def send(j, dx, dc):
            target = index_of(far_z(j), lax.rem(x + dx, NX), lax.rem(c + dc, NC))
            remote(buffer.at[target], recv.at[chain, order], ssem, rsem.at[chain], section, target)

        def farthest(j, carry):
            pack(j)
            send(j, 2, 1)
            send(j, 2, 0)
            return carry

        def middle(j, carry):
            for dx in (1, 3):
                send(j, dx, 1)
                send(j, dx, 0)
            return carry

        def line(j, carry):
            send(j, 0, 1)
            send(j, 0, 0)
            return carry

        lax.fori_loop(0, NZ, farthest, 0)
        lax.fori_loop(0, NZ, middle, 0)
        lax.fori_loop(0, NZ - 1, line, 0)
        send(NZ - 1, 0, 1)
        send_or_copy(buffer.at[e], recv.at[chain, order], ssem, rsem.at[chain], section, e, section == s)

    def give_back(ch, buffer, recv, rsem, ssem, in_plane, lap):
        def unpack(j):
            zz = far_z(j)
            block = pl.ds(pl.multiple_of(zz * NX * TILE, 64), NX * TILE)
            rows = jnp.concatenate([wide[0, block, :], wide[1, block, :]], axis=1).astype(BF16)
            buffer[ch, pl.ds(zz * NX, NX)] = rows.reshape(NX, TILE, LANES)

        def place_of(j, dx):
            zz, xx = far_z(j), lax.rem(x + dx, NX)
            section = jnp.where(in_plane, s, home_plane(zz, xx))
            return buffer.at[ch, zz * NX + xx], section, index_of(zz, xx, ch)

        def send(j, dx):
            src, section, target = place_of(j, dx)
            remote(src, recv.at[e], ssem, rsem, section, target)

        def farthest(j, carry):
            unpack(j)
            send(j, 2)
            return carry

        def middle(j, carry):
            send(j, 1)
            send(j, 3)
            return carry

        def line(j, carry):
            send(j, 0)
            return carry

        def rest():
            src, section, target = place_of(NZ - 1, 0)
            send_or_copy(src, recv.at[e], ssem, rsem, section, target, jnp.logical_and(section == s, ch == c))

        if lap is None:
            lax.fori_loop(0, NZ, farthest, 0)
            lax.fori_loop(0, NZ, middle, 0)
            lax.fori_loop(0, NZ - 1, line, 0)
            rest()
            return

        half = lap // (SECTIONS - 1)
        def gather(j, carry):
            unpack(j)
            zz = far_z(j)
            for k in range(SECTIONS - 1):
                xx = lax.rem(s + 1 + k + 2 * NZ - zz, NX)
                relay_send[ch, half, k, j - 5] = buffer[ch, zz * NX + xx]
            return carry

        lax.fori_loop(5, 7, gather, 0)
        for k in (1, 0, 2):
            remote(
                relay_send.at[ch, half, k], relay_recv.at[lap, ch], sent_relay, relay_sem.at[lap, ch],
                lax.rem(s + 1 + k, SECTIONS), e,
            )
        lax.fori_loop(0, 5, farthest, 0)
        lax.fori_loop(0, 5, middle, 0)
        lax.fori_loop(0, 5, line, 0)

        def near(j, carry):
            zz = far_z(j)
            xx = lax.rem(s + 2 * NZ - zz, NX)
            remote(buffer.at[ch, zz * NX + xx], recv.at[e], ssem, rsem, s, index_of(zz, xx, ch))
            return carry

        lax.fori_loop(5, 7, near, 0)
        unpack(NZ - 1)
        send(NZ - 1, 2)
        send(NZ - 1, 1)
        send(NZ - 1, 3)
        rest()

    def relay(lap, recv, rsem):
        def one(ch, carry):
            wait_all(relay_recv.at[lap, ch], relay_sem.at[lap, ch])

            def on(j, carry):
                zz = far_z(j)
                xx = lax.rem(s + 2 * NZ - zz, NX)
                remote(relay_recv.at[lap, ch, j - 5], recv.at[e], sent_on, rsem, s, index_of(zz, xx, ch))
                return carry

            lax.fori_loop(5, 7, on, 0)
            return carry

        lax.fori_loop(0, CHAINS, one, 0)

    loads[0].wait()
    loads[1].wait()
    loads[2].wait()
    loads[3].wait()
    loads[4].wait()
    note_own[0:TOKENS, 0:128] = route_info(ids_ref[...], wts_ref[...])
    note_own[0:TOKENS, 128:] = jnp.zeros((TOKENS, LANES - 128), F32)
    for p in range(PIECES):
        note_own[TOKENS + p : TOKENS + p + 1, :] = gain_ref[0:1, p * LANES : (p + 1) * LANES]
    own_info = note_own[0:TOKENS, 0:128]

    h_all[0] = to_pieces(x_ref).astype(BF16)

    @pl.when(first)
    def _():
        place_first[...] = place_matrix(own_info, False)

    g_all[SECTIONS] = to_pieces(og_ref).astype(BF16)

    @pl.when(last)
    def _():
        place_first[...] = place_matrix(own_info, True)

    pl.semaphore_wait(barrier, EXPERTS - 1 + SECTIONS - 1)

    def begin():
        scatter(place_first, h_all[0], send_first, f_recv, f_sem, sent_first, 0)

    @pl.when(jnp.logical_and(first, c == 0))
    def _():
        begin()

    @pl.when(last)
    def _():
        scatter(place_first, g_all[SECTIONS], send_first, b_recv, b_sem, sent_first, SECTIONS - 1)

    for k in range(1, SECTIONS):
        pl.semaphore_signal(planes_sem, inc=1, device_id=(lax.rem(s + k, SECTIONS), e), device_id_type=MESH)

    @pl.when(at_home)
    def _():
        notes[s] = note_own[...]

    @pl.when(jnp.logical_not(at_home))
    def _():
        remote(note_own, notes.at[s], sent_note, note_sem, home_plane(z, x), e)

    def dequant(code, steps, out, col, fan_in, groups):
        def one(g, carry):
            rows = pl.ds(pl.multiple_of(g * GROUP, GROUP), GROUP)
            scale = (steps[g] if len(steps.shape) == 3 else steps[pl.ds(g, 1), :]) * fan_in ** (-0.5)
            width = code.shape[1]
            out[rows, col : col + width] = ((code[rows, :].astype(F32) - 1.5) * scale).astype(BF16)
            return carry
        lax.fori_loop(0, groups, one, 0)

    loads[5].wait()
    loads[6].wait()
    dequant(gcode, gs_ref, w_gu, 0, WIDTH, WIDTH // GROUP)
    loads[7].wait()
    loads[8].wait()
    dequant(ucode, us_ref, w_gu, HIDDEN, WIDTH, WIDTH // GROUP)
    loads[9].wait()
    loads[10].wait()
    dequant(dcode, ds_ref, w_d, 0, HIDDEN, HIDDEN // GROUP)

    @pl.when(jnp.logical_and(first, c == 1))
    def _():
        begin()

    def info_of(layer):
        return notes[layer, 0:TOKENS, 0:128]

    pl.semaphore_wait(planes_sem, SECTIONS - 1)

    @pl.when(at_home)
    def _():
        wait_all(notes.at[pl.ds(0, SECTIONS - 1)], note_sem)
        take_w[0] = take_matrix(info_of(0), True)
        place_f[0] = place_matrix(info_of(1), False)

    def spread_out(recv, ch):
        flat = recv[ch].reshape(SOURCES * TILE, LANES).astype(F32)
        for half in range(2):
            wide[half] = flat[:, half * 128 : (half + 1) * 128]
        return [
            jnp.concatenate([wide[half, pl.ds(p, ROWS, stride=PIECES), :] for half in range(2)], axis=1)
            for p in range(PIECES)
        ]

    def collect(p, part):
        for half in range(2):
            wide[half, pl.ds(p, ROWS, stride=PIECES), :] = part[:, half * 128 : (half + 1) * 128]

    def rows_of(ch):
        return pl.ds(pl.multiple_of(ch * ROWS, ROWS), ROWS)

    def gates(ch):
        wait_all(f_recv.at[ch], f_sem.at[ch])
        parts = spread_out(f_recv, ch)
        square = functools.reduce(lambda a, b: a + b, [jnp.sum(q * q, axis=1, keepdims=True) for q in parts])
        inv = lax.rsqrt(square * (1.0 / WIDTH) + 1e-06)
        rows = rows_of(ch)
        for p in range(PIECES):
            lanes = slice(p * LANES, (p + 1) * LANES)
            x_rows[rows, lanes] = (parts[p] * inv * gain_ref[0:1, lanes]).astype(BF16)
        pre[rows, :] = dot(x_rows[rows, :], w_gu[...])
        gate, up = pre[rows, :HIDDEN], pre[rows, HIDDEN:]
        act[rows, :] = (gate * jax.nn.sigmoid(gate) * up).astype(BF16)

    def down(ch, lap):
        rows = rows_of(ch)
        for p in range(PIECES):
            collect(p, dot(act[rows, :], w_d[:, p * LANES : (p + 1) * LANES]))
        give_back(ch, r_send, r_recv, r_sem, sent_r, False, lap)

    def backward(ch):
        wait_all(b_recv.at[ch], b_sem.at[ch])
        parts = spread_out(b_recv, ch)
        rows = rows_of(ch)
        for p in range(PIECES):
            cot[rows, p * LANES : (p + 1) * LANES] = parts[p].astype(BF16)
        act_cot = dot(cot[rows, :], w_d[...], NT)
        gate, up = pre[rows, :HIDDEN], pre[rows, HIDDEN:]
        sig = jax.nn.sigmoid(gate)
        gu_cot[rows, :HIDDEN] = (act_cot * up * sig * (1.0 + gate * (1.0 - sig))).astype(BF16)
        gu_cot[rows, HIDDEN:] = (act_cot * gate * sig).astype(BF16)
        for p in range(PIECES):
            collect(p, dot(gu_cot[rows, :], w_gu[p * LANES : (p + 1) * LANES, :], NT))

        @pl.when(first)
        def _():
            give_back(ch, q_send, q_recv, q_sem, sent_q, True, None)

        @pl.when(s > 0)
        def _():
            give_back(ch, q_send, q_recv, q_sem, sent_q, False, SECTIONS - 2 + s)

    def home_forward(layer):
        wait_all(r_recv, r_sem)
        mixed = dot(take_w[layer], r_recv[...].reshape(EXPERTS * TILE, LANES))
        h_all[layer + 1] = (h_all[layer].astype(F32) + mixed).astype(BF16)

    def hand_output(layer):
        send_or_copy(h_all.at[layer + 1], lo_buf, sent_lo, lo_sem, layer, e, s == layer)

    def norm_back(matrix, hidden, gain8, above):
        wait_all(q_recv, q_sem)
        normed_cot = dot(matrix, q_recv[...].reshape(EXPERTS * TILE, LANES))
        hidden = hidden.astype(F32)
        inv = lax.rsqrt(token_sum(hidden * hidden) * (1.0 / WIDTH) + 1e-06)
        gain = jnp.broadcast_to(gain8.reshape(1, PIECES, LANES), (TOKENS, PIECES, LANES))
        scaled = gain.reshape(TOKENS * PIECES, LANES) * normed_cot
        mean = token_sum(scaled * hidden) * (1.0 / WIDTH)
        total = above.astype(F32) + inv * scaled - hidden * (inv * inv * inv) * mean
        return total.astype(BF16)

    def home_backward(layer):
        gain8 = notes[layer, TOKENS : TOKENS + PIECES, :]
        g_all[layer] = norm_back(take_1[layer - 1], h_all[layer], gain8, g_all[layer + 1])
        k = SECTIONS - 2 + layer
        scatter(place_b.at[layer - 1], g_all[layer], send_home.at[k], b_recv, b_sem, sent_home.at[k], layer - 1)
        send_or_copy(g_all.at[layer], ig_buf, sent_ig, ig_sem, layer, e, s == layer)

        @pl.when(layer == 1)
        def _():
            send_or_copy(g_all.at[layer], g1_buf, sent_g1, g1_sem, 0, e, s == 0)

        @pl.when(layer > 1)
        def _():
            prepare_back(layer - 1)

    def prepare_back(layer):
        take_1[layer - 1] = take_matrix(info_of(layer), False)
        place_b[layer - 1] = place_matrix(info_of(layer - 1), True)

    def step_grads():
        def gate_up(i, carry):
            rows = pl.ds(pl.multiple_of(i * 256, 256), 256)
            for code, out, col in ((gcode, gg_ref, 0), (ucode, ug_ref, HIDDEN)):
                grad = dot(x_rows[:, rows], gu_cot[:, col : col + HIDDEN], TN)
                grad = grad * (code[rows, :].astype(F32) - 1.5)
                summed = jnp.sum(grad.reshape(256 // GROUP, GROUP, HIDDEN), axis=1) * WIDTH ** (-0.5)
                for g in range(256 // GROUP):
                    out[pl.ds(i * (256 // GROUP) + g, 1), :] = summed[g : g + 1, :]
            return carry

        lax.fori_loop(0, WIDTH // 256, gate_up, 0)

        def down_part(i, carry):
            rows = pl.ds(pl.multiple_of(i * 256, 256), 256)
            for col in range(0, WIDTH, 1024):
                grad = dot(act[:, rows], cot[:, col : col + 1024], TN)
                grad = grad * (dcode[rows, col : col + 1024].astype(F32) - 1.5)
                summed = jnp.sum(grad.reshape(256 // GROUP, GROUP, 1024), axis=1) * HIDDEN ** (-0.5)
                for g in range(256 // GROUP):
                    dg_ref[i * (256 // GROUP) + g, :, col : col + 1024] = summed[g : g + 1, :]
            return carry

        lax.fori_loop(0, HIDDEN // 256, down_part, 0)

    def forward_layer(layer, carry):
        @pl.when(s == layer)
        def _():
            def expert(ch, carry):
                gates(ch)
                down(ch, layer)
                return carry

            lax.fori_loop(0, CHAINS, expert, 0)

        @pl.when(s != layer)
        def _():
            relay(layer, r_recv, r_sem)

        @pl.when(at_home)
        def _():
            home_forward(layer)
            scatter(
                place_f.at[layer], h_all[layer + 1], send_home.at[layer], f_recv, f_sem, sent_home.at[layer], layer + 1
            )
            hand_output(layer)
            take_w[layer + 1] = take_matrix(info_of(layer + 1), True)

            @pl.when(layer < SECTIONS - 2)
            def _():
                place_f[layer + 1] = place_matrix(info_of(layer + 2), False)

            @pl.when(layer == SECTIONS - 2)
            def _():
                prepare_back(SECTIONS - 1)

        return carry

    lax.fori_loop(0, SECTIONS - 1, forward_layer, 0)

    @pl.when(first)
    def _():
        take_last[...] = take_matrix(own_info, False)

    def backward_layer(t, carry):
        layer = SECTIONS - 1 - t

        @pl.when(s == layer)
        def _():
            def expert(ch, carry):
                @pl.when(last)
                def _():
                    gates(ch)

                backward(ch)
                return carry

            lax.fori_loop(0, CHAINS, expert, 0)

        @pl.when(jnp.logical_and(s != layer, layer > 0))
        def _():
            relay(SECTIONS - 2 + layer, q_recv, q_sem)

        @pl.when(jnp.logical_and(at_home, layer > 0))
        def _():
            home_backward(layer)

        @pl.when(jnp.logical_and(last, layer == SECTIONS - 1))
        def _():
            def give(ch, carry):
                down(ch, None)
                return carry

            lax.fori_loop(0, CHAINS, give, 0)

        @pl.when(s == layer)
        def _():
            step_grads()

        @pl.when(jnp.logical_and(at_home, t == 1))
        def _():
            home_forward(SECTIONS - 1)
            hand_output(SECTIONS - 1)

        return carry

    lax.fori_loop(0, SECTIONS, backward_layer, 0)

    wait_all(lo_buf, lo_sem)
    from_pieces(lo_buf[...].astype(F32), lo_ref)

    @pl.when(first)
    def _():
        wait_all(g1_buf, g1_sem)
        gain8 = note_own[TOKENS : TOKENS + PIECES, :]
        g_final[...] = norm_back(take_last[...], h_all[0], gain8, g1_buf[...])
        from_pieces(g_final[...].astype(F32), ig_ref)

    @pl.when(s > 0)
    def _():
        wait_all(ig_buf, ig_sem)
        from_pieces(ig_buf[...].astype(F32), ig_ref)

    def wait_messages(sem, some, own):
        @pl.when(own)
        def _():
            wait_all(some.at[pl.ds(0, EXPERTS - 1)], sem)

        @pl.when(jnp.logical_not(own))
        def _():
            wait_all(some, sem)

    @pl.when(jnp.logical_or(first, last))
    def _():
        wait_all(send_first.at[pl.ds(0, EXPERTS - 1)], sent_first)

    own = jnp.where(at_home, 1, 0)

    def wait_count(sem, count):
        def one(k, carry):
            wait_all(send_first.at[0], sem)
            return carry

        lax.fori_loop(0, count, one, 0)

    direct, ways = 26 * CHAINS, (SECTIONS - 1) * CHAINS
    wait_count(sent_r, jnp.where(last, EXPERTS, direct) - own)
    wait_count(sent_q, jnp.where(first, EXPERTS - 1, direct - own))
    wait_count(sent_relay, jnp.where(jnp.logical_or(first, last), 1, 2) * (2 * ways))
    wait_count(sent_on, 2 * CHAINS * jnp.where(first, 2 + 3, jnp.where(last, 3 + 2, 2 + 2)))

    @pl.when(jnp.logical_not(at_home))
    def _():
        wait_all(note_own, sent_note)

    @pl.when(at_home)
    def _():
        for layer in range(SECTIONS - 1):
            wait_messages(sent_home.at[layer], send_first, s == layer + 1)
            wait_messages(sent_home.at[SECTIONS - 1 + layer], send_first, s == layer)
        wait_all(h_all.at[pl.ds(0, SECTIONS - 1)], sent_lo)

        @pl.when(first)
        def _():
            wait_all(g_all.at[pl.ds(0, SECTIONS - 1)], sent_ig)

        @pl.when(s > 0)
        def _():
            wait_all(g_all.at[pl.ds(0, SECTIONS - 2)], sent_ig)
            wait_all(g1_buf, sent_g1)


def give_out(*refs):
    count = len(refs) // 3
    taken, given, held, sems = refs[:count], refs[count : 2 * count], refs[2 * count : 3 * count], refs[-1]
    loads = [pltpu.make_async_copy(taken[k], held[k], sems.at[0, k]) for k in range(count)]
    stores = [pltpu.make_async_copy(held[k], given[k], sems.at[1, k]) for k in range(count)]
    for load in loads:
        load.start()
    for load, store in zip(loads, stores):
        load.wait()
        store.start()
    for store in stores:
        store.wait()


def body(inputs, norm_gain, expert_ids, route_weights, gate_codes, up_codes, down_codes, gate_steps, up_steps, down_steps, out_grad):
    vmem = pl.BlockSpec(memory_space=pltpu.VMEM)
    hbm = pl.BlockSpec(memory_space=pl.ANY)
    message = (TILE, LANES)
    pieces = (TOKENS * PIECES, LANES)
    slots = EXPERTS * TILE
    both = CHAINS * ROWS
    steps = SECTIONS - 1
    tokens = (TOKENS, WIDTH)
    gate_shape, down_shape = (WIDTH, HIDDEN), (HIDDEN, WIDTH)
    gate_steps_shape, down_steps_shape = (WIDTH // GROUP, HIDDEN), (HIDDEN // GROUP, WIDTH)
    place, take = (slots, TOKENS * PIECES), (TOKENS * PIECES, slots)
    dma = pltpu.SemaphoreType.DMA
    scratch = [
        pltpu.VMEM(tokens, BF16),
        pltpu.VMEM(tokens, BF16),
        pltpu.VMEM((1, WIDTH), F32),
        pltpu.VMEM((TOP, TOKENS), jnp.int32),
        pltpu.VMEM((TOP, TOKENS), F32),
        pltpu.VMEM(gate_steps_shape, F32),
        pltpu.VMEM(gate_steps_shape, F32),
        pltpu.VMEM((HIDDEN // GROUP, 1, WIDTH), F32),
        pltpu.VMEM(gate_shape, BF16),
        pltpu.VMEM(gate_shape, BF16),
        pltpu.VMEM(down_shape, BF16),
        pltpu.VMEM((WIDTH, 2 * HIDDEN), BF16),
        pltpu.VMEM(down_shape, BF16),
        pltpu.VMEM((CHAINS, SOURCES) + message, BF16),
        pltpu.VMEM((EXPERTS,) + message, BF16),
        pltpu.VMEM((CHAINS, SOURCES) + message, BF16),
        pltpu.VMEM((EXPERTS,) + message, BF16),
        pltpu.VMEM((EXPERTS,) + message, BF16),
        pltpu.VMEM((2 * steps, EXPERTS) + message, BF16),
        pltpu.VMEM((CHAINS, SOURCES) + message, BF16),
        pltpu.VMEM((CHAINS, SOURCES) + message, BF16),
        pltpu.VMEM((CHAINS, 2, steps, 2) + message, BF16),
        pltpu.VMEM((2 * steps, CHAINS, 2) + message, BF16),
        pltpu.VMEM(place, BF16),
        pltpu.VMEM((steps,) + place, BF16),
        pltpu.VMEM((steps,) + place, BF16),
        pltpu.VMEM((SECTIONS,) + take, BF16),
        pltpu.VMEM((steps,) + take, BF16),
        pltpu.VMEM(take, BF16),
        pltpu.VMEM((SECTIONS + 1,) + pieces, BF16),
        pltpu.VMEM((SECTIONS + 1,) + pieces, BF16),
        pltpu.VMEM(pieces, BF16),
        pltpu.VMEM(pieces, BF16),
        pltpu.VMEM(pieces, BF16),
        pltpu.VMEM(pieces, BF16),
        pltpu.VMEM((TOKENS + PIECES, LANES), F32),
        pltpu.VMEM((SECTIONS, TOKENS + PIECES, LANES), F32),
        pltpu.VMEM((2, SOURCES * TILE, 128), F32),
        pltpu.VMEM((2, TOKENS * PIECES, 128), F32),
        pltpu.VMEM((both, WIDTH), BF16),
        pltpu.VMEM((both, 2 * HIDDEN), F32),
        pltpu.VMEM((both, HIDDEN), BF16),
        pltpu.VMEM((both, WIDTH), BF16),
        pltpu.VMEM((both, 2 * HIDDEN), BF16),
        dma((11,)),
        dma((CHAINS,)),
        dma,
        dma((CHAINS,)),
        dma,
        dma,
        dma,
        dma,
        dma,
        dma,
        dma((2 * steps,)),
        dma,
        dma,
        dma,
        dma,
        dma,
        dma,
        pltpu.SemaphoreType.REGULAR,
        dma((2 * steps, CHAINS)),
        dma,
        dma,
    ]
    outs = pl.pallas_call(
        kernel,
        out_shape=(
            jax.ShapeDtypeStruct(tokens, BF16),
            jax.ShapeDtypeStruct(tokens, BF16),
            jax.ShapeDtypeStruct(gate_steps_shape, F32),
            jax.ShapeDtypeStruct(gate_steps_shape, F32),
            jax.ShapeDtypeStruct((HIDDEN // GROUP, 1, WIDTH), F32),
        ),
        in_specs=[hbm] * 11,
        out_specs=[vmem] * 5,
        scratch_shapes=scratch,
        compiler_params=pltpu.CompilerParams(
            collective_id=0, has_side_effects=True, vmem_limit_bytes=58 * 1024 * 1024
        ),
    )(
        inputs[0], norm_gain, jnp.transpose(expert_ids[0, 0]), jnp.transpose(route_weights[0, 0]),
        gate_codes[0, 0], up_codes[0, 0], down_codes[0, 0],
        gate_steps[0, 0], up_steps[0, 0], jnp.transpose(down_steps[0], (1, 0, 2)), out_grad[0],
    )
    layer_out, input_grad, gate_grad, up_grad, down_grad = pl.pallas_call(
        give_out,
        out_shape=tuple(jax.ShapeDtypeStruct(out.shape, out.dtype) for out in outs),
        in_specs=[hbm] * len(outs),
        out_specs=[hbm] * len(outs),
        scratch_shapes=[pltpu.VMEM(out.shape, out.dtype) for out in outs] + [dma((2, len(outs)))],
    )(*outs)
    return (layer_out[None, None], input_grad[None, None], gate_grad[None, None], up_grad[None, None], jnp.transpose(down_grad, (1, 0, 2))[None])


def solution(mesh):
    in_specs = (
        P(None, "expert", None),
        P("section", None),
        P("section", None, "expert", None),
        P("section", None, "expert", None),
        P("section", "expert", None, None),
        P("section", "expert", None, None),
        P("section", "expert", None, None),
        P("section", "expert", None, None),
        P("section", "expert", None, None),
        P("section", "expert", None, None),
        P(None, "expert", None),
    )
    out_specs = (
        P("section", None, "expert", None),
        P("section", None, "expert", None),
        P("section", "expert", None, None),
        P("section", "expert", None, None),
        P("section", "expert", None, None),
    )
    return jax.shard_map(body, mesh=mesh, in_specs=in_specs, out_specs=out_specs, check_vma=False)
```

```python
import functools

import jax
import jax.numpy as jnp
from jax import lax
from jax.experimental import pallas as pl
from jax.experimental.pallas import tpu as pltpu
from jax.sharding import PartitionSpec as P

MESH = pl.DeviceIdType.MESH
BF16 = jnp.bfloat16
F32 = jnp.float32

SECTIONS, NZ, NX, NC = 4, 8, 4, 2
EXPERTS = NZ * NX * NC
TOKENS, TOP, SLOTS = 32, 2, 2
WIDTH, HIDDEN, GROUP = 2048, 768, 64
PIECES, LANES = 8, 256
TILE = SLOTS * PIECES
CHAINS = 2
SOURCES = EXPERTS // CHAINS
ROWS = SOURCES * SLOTS

NT = (((1,), (1,)), ((), ()))
TN = (((0,), (0,)), ((), ()))


def dot(a, b, dims=(((1,), (0,)), ((), ()))):
    return lax.dot_general(a, b, dims, preferred_element_type=F32)


def iota(shape, dim):
    return lax.broadcasted_iota(jnp.int32, shape, dim)


def route_info(ids, weights):
    lane = iota((TOKENS, 128), 1)
    same = iota((TOKENS, TOKENS), 0) == iota((TOKENS, TOKENS), 1)
    first, second = [jnp.sum(jnp.where(same, ids[k : k + 1, :], 0), axis=1, keepdims=True) for k in range(TOP)]
    weight0, weight1 = [jnp.sum(jnp.where(same, weights[k : k + 1, :], 0.0), axis=1, keepdims=True) for k in range(TOP)]
    hot0 = (lane == first).astype(F32)
    hot1 = (lane == second).astype(F32)
    earlier = (iota((TOKENS, TOKENS), 1) < iota((TOKENS, TOKENS), 0)).astype(BF16)
    count = dot(earlier, (hot0 + hot1).astype(BF16))
    slot0 = first.astype(F32) * SLOTS + jnp.sum(hot0 * count, axis=1, keepdims=True)
    slot1 = second.astype(F32) * SLOTS + jnp.sum(hot1 * count, axis=1, keepdims=True)
    info = jnp.where(lane == 0, slot0, 0.0) + jnp.where(lane == 1, slot1, 0.0)
    info = info + jnp.where(lane == 2, weight0, 0.0)
    return info + jnp.where(lane == 3, weight1, 0.0)


def place_matrix(info, weighted):
    spread = (iota((TOKENS, TOKENS * PIECES), 1) // PIECES == iota((TOKENS, TOKENS * PIECES), 0)).astype(BF16)
    cols = dot(info.astype(BF16), spread, TN)
    shape = (EXPERTS * TILE, TOKENS * PIECES)
    piece = iota((1, TOKENS * PIECES), 1) % PIECES
    at0 = cols[0:1, :].astype(jnp.int32) * PIECES + piece
    at1 = cols[1:2, :].astype(jnp.int32) * PIECES + piece
    row = iota(shape, 0)
    w0, w1 = (cols[2:3, :], cols[3:4, :]) if weighted else (1.0, 1.0)
    return (jnp.where(row == at0, w0, 0.0) + jnp.where(row == at1, w1, 0.0)).astype(BF16)


def take_matrix(info, weighted):
    spread = (iota((TOKENS * PIECES, TOKENS), 0) // PIECES == iota((TOKENS * PIECES, TOKENS), 1)).astype(BF16)
    rows = dot(spread, info.astype(BF16))
    shape = (TOKENS * PIECES, EXPERTS * TILE)
    piece = iota((TOKENS * PIECES, 1), 0) % PIECES
    at0 = rows[:, 0:1].astype(jnp.int32) * PIECES + piece
    at1 = rows[:, 1:2].astype(jnp.int32) * PIECES + piece
    col = iota(shape, 1)
    w0, w1 = (rows[:, 2:3], rows[:, 3:4]) if weighted else (1.0, 1.0)
    return (jnp.where(col == at0, w0, 0.0) + jnp.where(col == at1, w1, 0.0)).astype(BF16)


def token_sum(values):
    shaped = values.reshape(TOKENS, PIECES, LANES)
    total = jnp.sum(jnp.sum(shaped, axis=2, keepdims=True), axis=1, keepdims=True)
    return jnp.broadcast_to(total, (TOKENS, PIECES, LANES)).reshape(TOKENS * PIECES, LANES)


def home_plane(z, x):
    return lax.rem(z + x, SECTIONS)


def kernel(
    x_hbm, gain_hbm, ids_hbm, wts_hbm, gc_hbm, uc_hbm, dc_hbm, gs_hbm, us_hbm, ds_hbm, og_hbm,
    lo_ref, ig_ref, gg_ref, ug_ref, dg_ref,
    x_ref, og_ref, gain_ref, ids_ref, wts_ref, gs_ref, us_ref, ds_ref,
    gcode, ucode, dcode, w_gu, w_d,
    f_recv, r_recv, b_recv, q_recv, send_first, send_home, r_send, q_send, relay_send, relay_recv,
    place_first, place_f, place_b, take_w, take_1, take_last,
    h_all, g_all, g_final, lo_buf, ig_buf, g1_buf, note_own, notes,
    wide, home, x_rows, pre, act, cot, gu_cot,
    load_sem, f_sem, r_sem, b_sem, q_sem, note_sem, lo_sem, ig_sem, g1_sem,
    sent_first, sent_home, sent_r, sent_q, sent_note, sent_lo, sent_ig, sent_g1, planes_sem, relay_sem, sent_relay, sent_on,
):
    s = lax.axis_index("section")
    e = lax.axis_index("expert")
    z, x, c = e // (NX * NC), (e // NC) % NX, e % NC
    first, last = s == 0, s == SECTIONS - 1
    at_home = s == home_plane(z, x)

    def index_of(zz, xx, cc):
        return (zz * NX + xx) * NC + cc

    barrier = pltpu.get_barrier_semaphore()

    def greet(k, carry):
        pl.semaphore_signal(barrier, inc=1, device_id=(s, lax.rem(e + k, EXPERTS)), device_id_type=MESH)
        return carry

    lax.fori_loop(1, EXPERTS, greet, 0)
    for k in range(1, SECTIONS):
        pl.semaphore_signal(barrier, inc=1, device_id=(lax.rem(s + k, SECTIONS), e), device_id_type=MESH)

    pairs = [
        (ids_hbm, ids_ref), (wts_hbm, wts_ref), (x_hbm, x_ref), (gain_hbm, gain_ref), (og_hbm, og_ref),
        (gs_hbm, gs_ref), (gc_hbm, gcode), (us_hbm, us_ref), (uc_hbm, ucode), (ds_hbm, ds_ref), (dc_hbm, dcode),
    ]
    loads = [pltpu.make_async_copy(src, dst, load_sem.at[k]) for k, (src, dst) in enumerate(pairs)]
    for load in loads:
        load.start()

    def to_pieces(source):
        for p in range(PIECES):
            part = source[:, p * LANES : (p + 1) * LANES].astype(F32)
            for half in range(2):
                home[half, pl.ds(p, TOKENS, stride=PIECES), :] = part[:, half * 128 : (half + 1) * 128]
        return jnp.concatenate([home[0], home[1]], axis=1)

    def from_pieces(values, out_ref):
        for half in range(2):
            home[half] = values[:, half * 128 : (half + 1) * 128]
        for p in range(PIECES):
            for half in range(2):
                lanes = pl.ds(p * LANES + half * 128, 128)
                out_ref[:, lanes] = home[half, pl.ds(p, TOKENS, stride=PIECES), :].astype(out_ref.dtype)

    def far_z(j):
        return lax.rem(z + jnp.where(j % 2 == 0, 4 + j // 2, 3 - j // 2), NZ)

    def remote(src, dst, ssem, rsem, section, target):
        pltpu.make_async_remote_copy(
            src_ref=src, dst_ref=dst, send_sem=ssem, recv_sem=rsem, device_id=(section, target), device_id_type=MESH
        ).start()

    def send_or_copy(src, dst, ssem, rsem, section, target, own):
        @pl.when(own)
        def _():
            pltpu.make_async_copy(src, dst, rsem).start()

        @pl.when(jnp.logical_not(own))
        def _():
            remote(src, dst, ssem, rsem, section, target)

    def wait_all(ref, sem):
        pltpu.make_async_copy(ref, ref, sem).wait()

    chain, order = c, z * NX + x

    def scatter(place, values, buffer, recv, rsem, ssem, section):
        def pack(j):
            zz = far_z(j)
            block = pl.ds(pl.multiple_of(zz * NX * NC * TILE, 128), NX * NC * TILE)
            packed = dot(place[block, :], values).astype(BF16)
            buffer[pl.ds(zz * NX * NC, NX * NC)] = packed.reshape(NX * NC, TILE, LANES)

        def send(j, dx, dc):
            target = index_of(far_z(j), lax.rem(x + dx, NX), lax.rem(c + dc, NC))
            remote(buffer.at[target], recv.at[chain, order], ssem, rsem.at[chain], section, target)

        def farthest(j, carry):
            pack(j)
            send(j, 2, 1)
            send(j, 2, 0)
            return carry

        def middle(j, carry):
            for dx in (1, 3):
                send(j, dx, 1)
                send(j, dx, 0)
            return carry

        def line(j, carry):
            send(j, 0, 1)
            send(j, 0, 0)
            return carry

        lax.fori_loop(0, NZ, farthest, 0)
        lax.fori_loop(0, NZ, middle, 0)
        lax.fori_loop(0, NZ - 1, line, 0)
        send(NZ - 1, 0, 1)
        send_or_copy(buffer.at[e], recv.at[chain, order], ssem, rsem.at[chain], section, e, section == s)

    def give_back(ch, buffer, recv, rsem, ssem, in_plane, lap):
        def unpack(j):
            zz = far_z(j)
            block = pl.ds(pl.multiple_of(zz * NX * TILE, 64), NX * TILE)
            rows = jnp.concatenate([wide[0, block, :], wide[1, block, :]], axis=1).astype(BF16)
            buffer[ch, pl.ds(zz * NX, NX)] = rows.reshape(NX, TILE, LANES)

        def place_of(j, dx):
            zz, xx = far_z(j), lax.rem(x + dx, NX)
            section = jnp.where(in_plane, s, home_plane(zz, xx))
            return buffer.at[ch, zz * NX + xx], section, index_of(zz, xx, ch)

        def send(j, dx):
            src, section, target = place_of(j, dx)
            remote(src, recv.at[e], ssem, rsem, section, target)

        def farthest(j, carry):
            unpack(j)
            send(j, 2)
            return carry

        def middle(j, carry):
            send(j, 1)
            send(j, 3)
            return carry

        def line(j, carry):
            send(j, 0)
            return carry

        def rest():
            src, section, target = place_of(NZ - 1, 0)
            send_or_copy(src, recv.at[e], ssem, rsem, section, target, jnp.logical_and(section == s, ch == c))

        if lap is None:
            lax.fori_loop(0, NZ, farthest, 0)
            lax.fori_loop(0, NZ, middle, 0)
            lax.fori_loop(0, NZ - 1, line, 0)
            rest()
            return

        half = lap // (SECTIONS - 1)
        def gather(j, carry):
            unpack(j)
            zz = far_z(j)
            for k in range(SECTIONS - 1):
                xx = lax.rem(s + 1 + k + 2 * NZ - zz, NX)
                relay_send[ch, half, k, j - 5] = buffer[ch, zz * NX + xx]
            return carry

        lax.fori_loop(5, 7, gather, 0)
        for k in (1, 0, 2):
            remote(
                relay_send.at[ch, half, k], relay_recv.at[lap, ch], sent_relay, relay_sem.at[lap, ch],
                lax.rem(s + 1 + k, SECTIONS), e,
            )
        lax.fori_loop(0, 5, farthest, 0)
        lax.fori_loop(0, 5, middle, 0)
        lax.fori_loop(0, 5, line, 0)

        def near(j, carry):
            zz = far_z(j)
            xx = lax.rem(s + 2 * NZ - zz, NX)
            remote(buffer.at[ch, zz * NX + xx], recv.at[e], ssem, rsem, s, index_of(zz, xx, ch))
            return carry

        lax.fori_loop(5, 7, near, 0)
        unpack(NZ - 1)
        send(NZ - 1, 2)
        send(NZ - 1, 1)
        send(NZ - 1, 3)
        rest()

    def relay(lap, recv, rsem):
        def one(ch, carry):
            wait_all(relay_recv.at[lap, ch], relay_sem.at[lap, ch])

            def on(j, carry):
                zz = far_z(j)
                xx = lax.rem(s + 2 * NZ - zz, NX)
                remote(relay_recv.at[lap, ch, j - 5], recv.at[e], sent_on, rsem, s, index_of(zz, xx, ch))
                return carry

            lax.fori_loop(5, 7, on, 0)
            return carry

        lax.fori_loop(0, CHAINS, one, 0)

    loads[0].wait()
    loads[1].wait()
    loads[2].wait()
    loads[3].wait()
    loads[4].wait()
    note_own[0:TOKENS, 0:128] = route_info(ids_ref[...], wts_ref[...])
    note_own[0:TOKENS, 128:] = jnp.zeros((TOKENS, LANES - 128), F32)
    for p in range(PIECES):
        note_own[TOKENS + p : TOKENS + p + 1, :] = gain_ref[0:1, p * LANES : (p + 1) * LANES]
    own_info = note_own[0:TOKENS, 0:128]

    h_all[0] = to_pieces(x_ref).astype(BF16)

    @pl.when(first)
    def _():
        place_first[...] = place_matrix(own_info, False)

    g_all[SECTIONS] = to_pieces(og_ref).astype(BF16)

    @pl.when(last)
    def _():
        place_first[...] = place_matrix(own_info, True)

    pl.semaphore_wait(barrier, EXPERTS - 1 + SECTIONS - 1)

    def begin():
        scatter(place_first, h_all[0], send_first, f_recv, f_sem, sent_first, 0)

    @pl.when(jnp.logical_and(first, c == 0))
    def _():
        begin()

    @pl.when(last)
    def _():
        scatter(place_first, g_all[SECTIONS], send_first, b_recv, b_sem, sent_first, SECTIONS - 1)

    for k in range(1, SECTIONS):
        pl.semaphore_signal(planes_sem, inc=1, device_id=(lax.rem(s + k, SECTIONS), e), device_id_type=MESH)

    @pl.when(at_home)
    def _():
        notes[s] = note_own[...]

    @pl.when(jnp.logical_not(at_home))
    def _():
        remote(note_own, notes.at[s], sent_note, note_sem, home_plane(z, x), e)

    def dequant(code, steps, out, col, fan_in, groups):
        def one(g, carry):
            rows = pl.ds(pl.multiple_of(g * GROUP, GROUP), GROUP)
            scale = (steps[g] if len(steps.shape) == 3 else steps[pl.ds(g, 1), :]) * fan_in ** (-0.5)
            width = code.shape[1]
            out[rows, col : col + width] = ((code[rows, :].astype(F32) - 1.5) * scale).astype(BF16)
            return carry
        lax.fori_loop(0, groups, one, 0)

    loads[5].wait()
    loads[6].wait()
    dequant(gcode, gs_ref, w_gu, 0, WIDTH, WIDTH // GROUP)
    loads[7].wait()
    loads[8].wait()
    dequant(ucode, us_ref, w_gu, HIDDEN, WIDTH, WIDTH // GROUP)
    loads[9].wait()
    loads[10].wait()
    dequant(dcode, ds_ref, w_d, 0, HIDDEN, HIDDEN // GROUP)

    @pl.when(jnp.logical_and(first, c == 1))
    def _():
        begin()

    def info_of(layer):
        return notes[layer, 0:TOKENS, 0:128]

    pl.semaphore_wait(planes_sem, SECTIONS - 1)

    @pl.when(at_home)
    def _():
        wait_all(notes.at[pl.ds(0, SECTIONS - 1)], note_sem)
        take_w[0] = take_matrix(info_of(0), True)
        place_f[0] = place_matrix(info_of(1), False)

    def spread_out(recv, ch):
        flat = recv[ch].reshape(SOURCES * TILE, LANES).astype(F32)
        for half in range(2):
            wide[half] = flat[:, half * 128 : (half + 1) * 128]
        return [
            jnp.concatenate([wide[half, pl.ds(p, ROWS, stride=PIECES), :] for half in range(2)], axis=1)
            for p in range(PIECES)
        ]

    def collect(p, part):
        for half in range(2):
            wide[half, pl.ds(p, ROWS, stride=PIECES), :] = part[:, half * 128 : (half + 1) * 128]

    def rows_of(ch):
        return pl.ds(pl.multiple_of(ch * ROWS, ROWS), ROWS)

    def gates(ch):
        wait_all(f_recv.at[ch], f_sem.at[ch])
        parts = spread_out(f_recv, ch)
        square = functools.reduce(lambda a, b: a + b, [jnp.sum(q * q, axis=1, keepdims=True) for q in parts])
        inv = lax.rsqrt(square * (1.0 / WIDTH) + 1e-06)
        rows = rows_of(ch)
        for p in range(PIECES):
            lanes = slice(p * LANES, (p + 1) * LANES)
            x_rows[rows, lanes] = (parts[p] * inv * gain_ref[0:1, lanes]).astype(BF16)
        pre[rows, :] = dot(x_rows[rows, :], w_gu[...])
        gate, up = pre[rows, :HIDDEN], pre[rows, HIDDEN:]
        act[rows, :] = (gate * jax.nn.sigmoid(gate) * up).astype(BF16)

    def down(ch, lap):
        rows = rows_of(ch)
        for p in range(PIECES):
            collect(p, dot(act[rows, :], w_d[:, p * LANES : (p + 1) * LANES]))
        give_back(ch, r_send, r_recv, r_sem, sent_r, False, lap)

    def backward(ch):
        wait_all(b_recv.at[ch], b_sem.at[ch])
        parts = spread_out(b_recv, ch)
        rows = rows_of(ch)
        for p in range(PIECES):
            cot[rows, p * LANES : (p + 1) * LANES] = parts[p].astype(BF16)
        act_cot = dot(cot[rows, :], w_d[...], NT)
        gate, up = pre[rows, :HIDDEN], pre[rows, HIDDEN:]
        sig = jax.nn.sigmoid(gate)
        gu_cot[rows, :HIDDEN] = (act_cot * up * sig * (1.0 + gate * (1.0 - sig))).astype(BF16)
        gu_cot[rows, HIDDEN:] = (act_cot * gate * sig).astype(BF16)
        for p in range(PIECES):
            collect(p, dot(gu_cot[rows, :], w_gu[p * LANES : (p + 1) * LANES, :], NT))

        @pl.when(first)
        def _():
            give_back(ch, q_send, q_recv, q_sem, sent_q, True, None)

        @pl.when(s > 0)
        def _():
            give_back(ch, q_send, q_recv, q_sem, sent_q, False, SECTIONS - 2 + s)

    def home_forward(layer):
        wait_all(r_recv, r_sem)
        mixed = dot(take_w[layer], r_recv[...].reshape(EXPERTS * TILE, LANES))
        h_all[layer + 1] = (h_all[layer].astype(F32) + mixed).astype(BF16)

    def hand_output(layer):
        send_or_copy(h_all.at[layer + 1], lo_buf, sent_lo, lo_sem, layer, e, s == layer)

    def norm_back(matrix, hidden, gain8, above):
        hidden = hidden.astype(F32)
        inv = lax.rsqrt(token_sum(hidden * hidden) * (1.0 / WIDTH) + 1e-06)
        wait_all(q_recv, q_sem)
        normed_cot = dot(matrix, q_recv[...].reshape(EXPERTS * TILE, LANES))
        gain = jnp.broadcast_to(gain8.reshape(1, PIECES, LANES), (TOKENS, PIECES, LANES))
        scaled = gain.reshape(TOKENS * PIECES, LANES) * normed_cot
        mean = token_sum(scaled * hidden) * (1.0 / WIDTH)
        total = above.astype(F32) + inv * scaled - hidden * (inv * inv * inv) * mean
        return total.astype(BF16)

    def home_backward(layer):
        gain8 = notes[layer, TOKENS : TOKENS + PIECES, :]
        g_all[layer] = norm_back(take_1[layer - 1], h_all[layer], gain8, g_all[layer + 1])
        k = SECTIONS - 2 + layer
        scatter(place_b.at[layer - 1], g_all[layer], send_home.at[k], b_recv, b_sem, sent_home.at[k], layer - 1)
        send_or_copy(g_all.at[layer], ig_buf, sent_ig, ig_sem, layer, e, s == layer)

        @pl.when(layer == 1)
        def _():
            send_or_copy(g_all.at[layer], g1_buf, sent_g1, g1_sem, 0, e, s == 0)

        @pl.when(layer > 1)
        def _():
            prepare_back(layer - 1)

    def prepare_back(layer):
        take_1[layer - 1] = take_matrix(info_of(layer), False)
        place_b[layer - 1] = place_matrix(info_of(layer - 1), True)

    def step_grads():
        def gate_up(i, carry):
            rows = pl.ds(pl.multiple_of(i * 256, 256), 256)
            for code, out, col in ((gcode, gg_ref, 0), (ucode, ug_ref, HIDDEN)):
                grad = dot(x_rows[:, rows], gu_cot[:, col : col + HIDDEN], TN)
                grad = grad * (code[rows, :].astype(F32) - 1.5)
                summed = jnp.sum(grad.reshape(256 // GROUP, GROUP, HIDDEN), axis=1) * WIDTH ** (-0.5)
                for g in range(256 // GROUP):
                    out[pl.ds(i * (256 // GROUP) + g, 1), :] = summed[g : g + 1, :]
            return carry

        lax.fori_loop(0, WIDTH // 256, gate_up, 0)

        def down_part(i, carry):
            rows = pl.ds(pl.multiple_of(i * 256, 256), 256)
            for col in range(0, WIDTH, 1024):
                grad = dot(act[:, rows], cot[:, col : col + 1024], TN)
                grad = grad * (dcode[rows, col : col + 1024].astype(F32) - 1.5)
                summed = jnp.sum(grad.reshape(256 // GROUP, GROUP, 1024), axis=1) * HIDDEN ** (-0.5)
                for g in range(256 // GROUP):
                    dg_ref[i * (256 // GROUP) + g, :, col : col + 1024] = summed[g : g + 1, :]
            return carry

        lax.fori_loop(0, HIDDEN // 256, down_part, 0)

    def forward_layer(layer, carry):
        @pl.when(s == layer)
        def _():
            def expert(ch, carry):
                gates(ch)
                down(ch, layer)
                return carry

            lax.fori_loop(0, CHAINS, expert, 0)

        @pl.when(s != layer)
        def _():
            relay(layer, r_recv, r_sem)

        @pl.when(at_home)
        def _():
            home_forward(layer)
            scatter(
                place_f.at[layer], h_all[layer + 1], send_home.at[layer], f_recv, f_sem, sent_home.at[layer], layer + 1
            )
            hand_output(layer)
            take_w[layer + 1] = take_matrix(info_of(layer + 1), True)

            @pl.when(layer < SECTIONS - 2)
            def _():
                place_f[layer + 1] = place_matrix(info_of(layer + 2), False)

            @pl.when(layer == SECTIONS - 2)
            def _():
                prepare_back(SECTIONS - 1)

        return carry

    lax.fori_loop(0, SECTIONS - 1, forward_layer, 0)

    @pl.when(first)
    def _():
        take_last[...] = take_matrix(own_info, False)

    def backward_layer(t, carry):
        layer = SECTIONS - 1 - t

        @pl.when(s == layer)
        def _():
            def expert(ch, carry):
                @pl.when(last)
                def _():
                    gates(ch)

                backward(ch)
                return carry

            lax.fori_loop(0, CHAINS, expert, 0)

        @pl.when(jnp.logical_and(s != layer, layer > 0))
        def _():
            relay(SECTIONS - 2 + layer, q_recv, q_sem)

        @pl.when(jnp.logical_and(at_home, layer > 0))
        def _():
            home_backward(layer)

        @pl.when(jnp.logical_and(last, layer == SECTIONS - 1))
        def _():
            def give(ch, carry):
                down(ch, None)
                return carry

            lax.fori_loop(0, CHAINS, give, 0)

        @pl.when(s == layer)
        def _():
            step_grads()

        @pl.when(jnp.logical_and(at_home, t == 1))
        def _():
            home_forward(SECTIONS - 1)
            hand_output(SECTIONS - 1)

        return carry

    lax.fori_loop(0, SECTIONS, backward_layer, 0)

    wait_all(lo_buf, lo_sem)
    from_pieces(lo_buf[...].astype(F32), lo_ref)

    @pl.when(first)
    def _():
        wait_all(g1_buf, g1_sem)
        gain8 = note_own[TOKENS : TOKENS + PIECES, :]
        g_final[...] = norm_back(take_last[...], h_all[0], gain8, g1_buf[...])
        from_pieces(g_final[...].astype(F32), ig_ref)

    @pl.when(s > 0)
    def _():
        wait_all(ig_buf, ig_sem)
        from_pieces(ig_buf[...].astype(F32), ig_ref)

    def wait_messages(sem, some, own):
        @pl.when(own)
        def _():
            wait_all(some.at[pl.ds(0, EXPERTS - 1)], sem)

        @pl.when(jnp.logical_not(own))
        def _():
            wait_all(some, sem)

    @pl.when(jnp.logical_or(first, last))
    def _():
        wait_all(send_first.at[pl.ds(0, EXPERTS - 1)], sent_first)

    own = jnp.where(at_home, 1, 0)

    def wait_count(sem, count):
        def one(k, carry):
            wait_all(send_first.at[0], sem)
            return carry

        lax.fori_loop(0, count, one, 0)

    direct, ways = 26 * CHAINS, (SECTIONS - 1) * CHAINS
    wait_count(sent_r, jnp.where(last, EXPERTS, direct) - own)
    wait_count(sent_q, jnp.where(first, EXPERTS - 1, direct - own))
    wait_count(sent_relay, jnp.where(jnp.logical_or(first, last), 1, 2) * (2 * ways))
    wait_count(sent_on, 2 * CHAINS * jnp.where(first, 2 + 3, jnp.where(last, 3 + 2, 2 + 2)))

    @pl.when(jnp.logical_not(at_home))
    def _():
        wait_all(note_own, sent_note)

    @pl.when(at_home)
    def _():
        for layer in range(SECTIONS - 1):
            wait_messages(sent_home.at[layer], send_first, s == layer + 1)
            wait_messages(sent_home.at[SECTIONS - 1 + layer], send_first, s == layer)
        wait_all(h_all.at[pl.ds(0, SECTIONS - 1)], sent_lo)

        @pl.when(first)
        def _():
            wait_all(g_all.at[pl.ds(0, SECTIONS - 1)], sent_ig)

        @pl.when(s > 0)
        def _():
            wait_all(g_all.at[pl.ds(0, SECTIONS - 2)], sent_ig)
            wait_all(g1_buf, sent_g1)


def give_out(*refs):
    count = len(refs) // 3
    taken, given, held, sems = refs[:count], refs[count : 2 * count], refs[2 * count : 3 * count], refs[-1]
    loads = [pltpu.make_async_copy(taken[k], held[k], sems.at[0, k]) for k in range(count)]
    stores = [pltpu.make_async_copy(held[k], given[k], sems.at[1, k]) for k in range(count)]
    for load in loads:
        load.start()
    for load, store in zip(loads, stores):
        load.wait()
        store.start()
    for store in stores:
        store.wait()


def body(inputs, norm_gain, expert_ids, route_weights, gate_codes, up_codes, down_codes, gate_steps, up_steps, down_steps, out_grad):
    vmem = pl.BlockSpec(memory_space=pltpu.VMEM)
    hbm = pl.BlockSpec(memory_space=pl.ANY)
    message = (TILE, LANES)
    pieces = (TOKENS * PIECES, LANES)
    slots = EXPERTS * TILE
    both = CHAINS * ROWS
    steps = SECTIONS - 1
    tokens = (TOKENS, WIDTH)
    gate_shape, down_shape = (WIDTH, HIDDEN), (HIDDEN, WIDTH)
    gate_steps_shape, down_steps_shape = (WIDTH // GROUP, HIDDEN), (HIDDEN // GROUP, WIDTH)
    place, take = (slots, TOKENS * PIECES), (TOKENS * PIECES, slots)
    dma = pltpu.SemaphoreType.DMA
    scratch = [
        pltpu.VMEM(tokens, BF16),
        pltpu.VMEM(tokens, BF16),
        pltpu.VMEM((1, WIDTH), F32),
        pltpu.VMEM((TOP, TOKENS), jnp.int32),
        pltpu.VMEM((TOP, TOKENS), F32),
        pltpu.VMEM(gate_steps_shape, F32),
        pltpu.VMEM(gate_steps_shape, F32),
        pltpu.VMEM((HIDDEN // GROUP, 1, WIDTH), F32),
        pltpu.VMEM(gate_shape, BF16),
        pltpu.VMEM(gate_shape, BF16),
        pltpu.VMEM(down_shape, BF16),
        pltpu.VMEM((WIDTH, 2 * HIDDEN), BF16),
        pltpu.VMEM(down_shape, BF16),
        pltpu.VMEM((CHAINS, SOURCES) + message, BF16),
        pltpu.VMEM((EXPERTS,) + message, BF16),
        pltpu.VMEM((CHAINS, SOURCES) + message, BF16),
        pltpu.VMEM((EXPERTS,) + message, BF16),
        pltpu.VMEM((EXPERTS,) + message, BF16),
        pltpu.VMEM((2 * steps, EXPERTS) + message, BF16),
        pltpu.VMEM((CHAINS, SOURCES) + message, BF16),
        pltpu.VMEM((CHAINS, SOURCES) + message, BF16),
        pltpu.VMEM((CHAINS, 2, steps, 2) + message, BF16),
        pltpu.VMEM((2 * steps, CHAINS, 2) + message, BF16),
        pltpu.VMEM(place, BF16),
        pltpu.VMEM((steps,) + place, BF16),
        pltpu.VMEM((steps,) + place, BF16),
        pltpu.VMEM((SECTIONS,) + take, BF16),
        pltpu.VMEM((steps,) + take, BF16),
        pltpu.VMEM(take, BF16),
        pltpu.VMEM((SECTIONS + 1,) + pieces, BF16),
        pltpu.VMEM((SECTIONS + 1,) + pieces, BF16),
        pltpu.VMEM(pieces, BF16),
        pltpu.VMEM(pieces, BF16),
        pltpu.VMEM(pieces, BF16),
        pltpu.VMEM(pieces, BF16),
        pltpu.VMEM((TOKENS + PIECES, LANES), F32),
        pltpu.VMEM((SECTIONS, TOKENS + PIECES, LANES), F32),
        pltpu.VMEM((2, SOURCES * TILE, 128), F32),
        pltpu.VMEM((2, TOKENS * PIECES, 128), F32),
        pltpu.VMEM((both, WIDTH), BF16),
        pltpu.VMEM((both, 2 * HIDDEN), F32),
        pltpu.VMEM((both, HIDDEN), BF16),
        pltpu.VMEM((both, WIDTH), BF16),
        pltpu.VMEM((both, 2 * HIDDEN), BF16),
        dma((11,)),
        dma((CHAINS,)),
        dma,
        dma((CHAINS,)),
        dma,
        dma,
        dma,
        dma,
        dma,
        dma,
        dma((2 * steps,)),
        dma,
        dma,
        dma,
        dma,
        dma,
        dma,
        pltpu.SemaphoreType.REGULAR,
        dma((2 * steps, CHAINS)),
        dma,
        dma,
    ]
    outs = pl.pallas_call(
        kernel,
        out_shape=(
            jax.ShapeDtypeStruct(tokens, BF16),
            jax.ShapeDtypeStruct(tokens, BF16),
            jax.ShapeDtypeStruct(gate_steps_shape, F32),
            jax.ShapeDtypeStruct(gate_steps_shape, F32),
            jax.ShapeDtypeStruct((HIDDEN // GROUP, 1, WIDTH), F32),
        ),
        in_specs=[hbm] * 11,
        out_specs=[vmem] * 5,
        scratch_shapes=scratch,
        compiler_params=pltpu.CompilerParams(
            collective_id=0, has_side_effects=True, vmem_limit_bytes=58 * 1024 * 1024
        ),
    )(
        inputs[0], norm_gain, jnp.transpose(expert_ids[0, 0]), jnp.transpose(route_weights[0, 0]),
        gate_codes[0, 0], up_codes[0, 0], down_codes[0, 0],
        gate_steps[0, 0], up_steps[0, 0], jnp.transpose(down_steps[0], (1, 0, 2)), out_grad[0],
    )
    layer_out, input_grad, gate_grad, up_grad, down_grad = pl.pallas_call(
        give_out,
        out_shape=tuple(jax.ShapeDtypeStruct(out.shape, out.dtype) for out in outs),
        in_specs=[hbm] * len(outs),
        out_specs=[hbm] * len(outs),
        scratch_shapes=[pltpu.VMEM(out.shape, out.dtype) for out in outs] + [dma((2, len(outs)))],
    )(*outs)
    return (layer_out[None, None], input_grad[None, None], gate_grad[None, None], up_grad[None, None], jnp.transpose(down_grad, (1, 0, 2))[None])


def solution(mesh):
    in_specs = (
        P(None, "expert", None),
        P("section", None),
        P("section", None, "expert", None),
        P("section", None, "expert", None),
        P("section", "expert", None, None),
        P("section", "expert", None, None),
        P("section", "expert", None, None),
        P("section", "expert", None, None),
        P("section", "expert", None, None),
        P("section", "expert", None, None),
        P(None, "expert", None),
    )
    out_specs = (
        P("section", None, "expert", None),
        P("section", None, "expert", None),
        P("section", "expert", None, None),
        P("section", "expert", None, None),
        P("section", "expert", None, None),
    )
    return jax.shard_map(body, mesh=mesh, in_specs=in_specs, out_specs=out_specs, check_vma=False)
```
